256 devices in a mesh: dp: 16 (over z_hi, y), expert: 16 (over z_lo, x, core).
Axes of the slice: x: 4, y: 4, z: 8 (z_hi: 4, z_lo: 2; z = z_hi * 2 + z_lo), core: 2. Of those that a mesh axis runs over, the one named last changes fastest.
Arguments:
- patches: bfloat16 [512, 256, 1280], P(('dp', 'expert')), may hold values from -12 to 12
- cotangent: bfloat16 [512, 256, 1280], P(('dp', 'expert')), may hold values from -6 to 6
- other_logsum: float32 [512, 256], P(('dp', 'expert')), may hold values from 6 to 9
- slot_keys: bfloat16 [32, 1280], replicated, may hold values from -0.25 to 0.25
- w_in: bfloat16 [32, 1280, 5120], P('expert', None, 'dp'), may hold values from -0.15625 to 0.15625
- w_out: bfloat16 [32, 5120, 1280], P('expert', 'dp'), may hold values from -0.078125 to 0.078125
Outputs:
- patch_grad: bfloat16 [512, 256, 1280], P(('dp', 'expert'))
- key_grad: float32 [32, 1280], replicated
- w_in_grad: bfloat16 [32, 1280, 5120], P('expert', None, 'dp')
- w_out_grad: bfloat16 [32, 5120, 1280], P('expert', 'dp')
The draws below stay inside these ranges and needn't reach their ends.
All inputs are finite; a program needn't handle non-finite values.
Results may differ from the reference program's by a relative error of at most 0.03.
Values may be sent and summed in bfloat16 or wider, within the bound.
A program may use at most 128 MiB of HBM per device.

```python
import jax
import jax.numpy as jnp
from jax import lax

D = 1280
FF = 5120
PATCHES = 256
EXPERTS = 32
IMAGES = 512
N_DP = 16


def block_levels(key, dims, cuts, low, top_value):
    def one(dim, shards_of):
        steps = jax.random.uniform(jax.random.fold_in(jax.random.fold_in(key, 6), dim), (shards_of,), jnp.float32, low / len(cuts), top_value / len(cuts))
        return jnp.repeat(jnp.exp(steps), dims[dim] // shards_of).reshape((-1,) + (1,) * (len(dims) - dim - 1))

    factor_of = one(*cuts[0])
    for cut in cuts[1:]:
        factor_of = factor_of * one(*cut)
    return factor_of


def normal_values(rng, shape, scale, limit, shards=(), kind=jnp.bfloat16):
    values = jax.random.normal(rng, shape, jnp.float32) * scale
    if len(shards) > 0:
        values = block_levels(rng, shape, shards, -0.22, 0.18) * values
    return jnp.clip(values, min=-limit, max=limit).astype(kind)


def setup_inputs(seed: int = 0) -> dict:
    key_list = jax.random.split(jax.random.key(seed), 7)
    return {
        "patches": normal_values(key_list[0], (IMAGES, PATCHES, D), 2.0, 12.0, ((0, 256),)),
        "cotangent": normal_values(key_list[1], (IMAGES, PATCHES, D), 1.0, 6.0, ((0, 256),)),
        "other_logsum": jnp.clip(6.0 + 3.0 * jax.random.uniform(key_list[2], (IMAGES, PATCHES), jnp.float32) ** block_levels(key_list[2], (IMAGES, PATCHES), ((0, 256),), -0.2, 0.2), 6.0, 9.0),
        "slot_keys": normal_values(key_list[3], (EXPERTS, D), (4 * D // 9) ** -0.5, 0.25),
        "w_in": normal_values(key_list[4], (EXPERTS, D, FF), D ** -0.5, 0.15625, ((0, 16), (2, 16))),
        "w_out": normal_values(key_list[5], (EXPERTS, FF, D), FF ** -0.5, 0.078125, ((0, 16), (1, 16))),
    }


def image_slots(x_img, g_img, rest_img, keys):
    logits = jnp.dot(keys, x_img.T, preferred_element_type=jnp.float32)
    exponent = jnp.exp(logits)
    dispatch = exponent / lax.optimization_barrier(jnp.sum(exponent, axis=1, keepdims=True))
    combine = exponent / (lax.optimization_barrier(jnp.sum(exponent, axis=0, keepdims=True)) + jnp.exp(rest_img)[None, :])
    dispatch_half = dispatch.astype(jnp.bfloat16)
    combine_half = combine.astype(jnp.bfloat16)
    slot_in = jnp.dot(dispatch_half, x_img, preferred_element_type=jnp.float32).astype(jnp.bfloat16)
    slot_grad = jnp.dot(combine_half, g_img, preferred_element_type=jnp.float32).astype(jnp.bfloat16)
    return (slot_in, slot_grad)

def one_expert(slot_rows, grad_rows, w_first, w_second):
    images = slot_rows.shape[0]
    block = w_first.shape[1] // N_DP
    hidden = jnp.dot(slot_rows, w_first, preferred_element_type=jnp.float32)
    upstream = jnp.dot(grad_rows, w_second.T, preferred_element_type=jnp.float32)
    activated, pullback = jax.vjp(jax.nn.gelu, hidden)
    act_half = activated.astype(jnp.bfloat16)
    pre_half = pullback(upstream)[0].astype(jnp.bfloat16)
    w_out_grad = jnp.dot(act_half.T, grad_rows, preferred_element_type=jnp.float32).astype(jnp.bfloat16)
    w_in_grad = jnp.dot(slot_rows.T, pre_half, preferred_element_type=jnp.float32).astype(jnp.bfloat16)
    act_blocks = act_half.astype(jnp.float32).reshape(images, N_DP, block)
    pre_blocks = pre_half.astype(jnp.float32).reshape(images, N_DP, block)
    second_blocks = w_second.astype(jnp.float32).reshape(N_DP, block, -1)
    first_blocks = w_first.astype(jnp.float32).reshape(-1, N_DP, block)
    out_parts = jnp.einsum('bkf,kfd->kbd', act_blocks, second_blocks)
    in_parts = jnp.einsum('bkf,dkf->kbd', pre_blocks, first_blocks)
    slot_out = lax.optimization_barrier(jnp.sum(out_parts.astype(jnp.bfloat16).astype(jnp.float32), axis=0)).astype(jnp.bfloat16)
    slot_in_grad = lax.optimization_barrier(jnp.sum(in_parts.astype(jnp.bfloat16).astype(jnp.float32), axis=0)).astype(jnp.bfloat16)
    return (slot_out, slot_in_grad, w_in_grad, w_out_grad)

def image_grads(x_img, g_img, rest_img, keys, slot_out, slot_in_grad):
    logits = jnp.dot(keys, x_img.T, preferred_element_type=jnp.float32)
    exponent = jnp.exp(logits)
    dispatch = exponent / lax.optimization_barrier(jnp.sum(exponent, axis=1, keepdims=True))
    combine = exponent / (lax.optimization_barrier(jnp.sum(exponent, axis=0, keepdims=True)) + jnp.exp(rest_img)[None, :])
    dispatch_half = dispatch.astype(jnp.bfloat16)
    comb_grad = jnp.dot(slot_out, g_img.T, preferred_element_type=jnp.float32)
    disp_grad = jnp.dot(slot_in_grad, x_img.T, preferred_element_type=jnp.float32)
    logit_grad = combine * (comb_grad - lax.optimization_barrier(jnp.sum(combine * comb_grad, axis=0, keepdims=True)))
    logit_grad = logit_grad + dispatch * (disp_grad - lax.optimization_barrier(jnp.sum(dispatch * disp_grad, axis=1, keepdims=True)))
    logit_half = logit_grad.astype(jnp.bfloat16)
    patch_grad = jnp.dot(dispatch_half.T, slot_in_grad, preferred_element_type=jnp.float32)
    patch_grad = patch_grad + jnp.dot(logit_half.T, keys, preferred_element_type=jnp.float32)
    key_part = jnp.dot(logit_half, x_img, preferred_element_type=jnp.float32)
    return (patch_grad.astype(jnp.bfloat16), key_part)

def reference(patches, cotangent, other_logsum, slot_keys, w_in, w_out):
    slot_in, slot_grad = lax.map(lambda items: image_slots(items[0], items[1], items[2], slot_keys), (patches, cotangent, other_logsum))
    slot_out, slot_in_grad, w_in_grad, w_out_grad = lax.map(lambda items: one_expert(items[0], items[1], items[2], items[3]), (jnp.transpose(slot_in, (1, 0, 2)), jnp.transpose(slot_grad, (1, 0, 2)), w_in, w_out))
    slot_out = jnp.transpose(slot_out, (1, 0, 2))
    slot_in_grad = jnp.transpose(slot_in_grad, (1, 0, 2))
    patch_grad, key_parts = lax.map(lambda items: image_grads(items[0], items[1], items[2], slot_keys, items[3], items[4]), (patches, cotangent, other_logsum, slot_out, slot_in_grad))
    key_grad = lax.optimization_barrier(jnp.sum(key_parts, axis=0))
    return (patch_grad, key_grad, w_in_grad, w_out_grad)
```

```python
import functools

import jax
import jax.numpy as jnp
from jax import lax
from jax.experimental import pallas as pl
from jax.experimental.pallas import tpu as pltpu
from jax.sharding import PartitionSpec as P

MESH = pl.DeviceIdType.MESH
BF = jnp.bfloat16
F32 = jnp.float32

D = 1280
FB = 320
SPLIT = 1024
COLS = ((0, SPLIT), (SPLIT, D - SPLIT))
N_SEM = 224
GELU_C = 0.7978845608028654
GELU_A = 0.044715


def dot(a, b):
    return lax.dot_general(a, b, (((1,), (0,)), ((), ())), preferred_element_type=F32)


def dot_nt(a, b):
    return lax.dot_general(a, b, (((1,), (1,)), ((), ())), preferred_element_type=F32)


def dot_tn(a, b):
    return lax.dot_general(a, b, (((0,), (0,)), ((), ())), preferred_element_type=F32)


def iota(shape, dim):
    return lax.broadcasted_iota(jnp.int32, shape, dim)


def piece_row(slot_off, half, k, t, i):
    return slot_off * 16 + half * 8 + k * 4 + t * 2 + i


def spread_index(r, me):
    off, k, t, i = r >> 4, (r >> 2) & 1, (r >> 1) & 1, r & 1
    owner = (me + off) & 15
    return (t * 2 + i) * 32 + 2 * owner + k


def block_index(r):
    off, k, t, i = r >> 4, (r >> 2) & 1, (r >> 1) & 1, r & 1
    return (k * 2 + t) * 32 + off * 2 + i


def one_hot(index_of, half, rows_are_pieces):
    shape = (256, 128) if rows_are_pieces else (128, 256)
    piece = iota(shape, 0 if rows_are_pieces else 1)
    other = iota(shape, 1 if rows_are_pieces else 0)
    hit = (index_of(piece) == other) & (((piece >> 3) & 1) == half)
    return jnp.where(hit, 1.0, 0.0).astype(BF)


def kernel(
    patches_hbm, cot_hbm, ols_ref, keys_ref, win_hbm, wout_hbm,
    pg_hbm, kg_ref, wig_hbm, wog_hbm,
    patches, cot, win, wout, pg, wig, wog,
    disp_s, comb_s, g, pt, act_s, pre_s, r1, r2,
    a2s, a2r, b2s, b2r, ks, k1, k2, k3, k4,
    send_sem, recv_sem, in_sem, out_sem,
):
    dp = lax.axis_index("dp")
    me = lax.axis_index("expert")
    zh, y = dp // 4, dp % 4

    def expert_peer(off):
        return (dp, lax.rem(me + off, 16))

    def dp_peer(off):
        return (lax.rem(dp + off, 16), me)

    def ring_peer(axis, step):
        if axis == "y":
            return (zh * 4 + lax.rem(y + step + 4, 4), me)
        return (lax.rem(zh + step + 4, 4) * 4 + y, me)

    barrier = pltpu.get_barrier_semaphore()
    for off in range(1, 16):
        pl.semaphore_signal(barrier, inc=1, device_id=expert_peer(off), device_id_type=MESH)
        pl.semaphore_signal(barrier, inc=1, device_id=dp_peer(off), device_id_type=MESH)

    loads = {}
    for n, (name, src, dst) in enumerate(
        (("x", patches_hbm, patches), ("c", cot_hbm, cot), ("wi", win_hbm, win), ("wo", wout_hbm, wout))
    ):
        loads[name] = pltpu.make_async_copy(src, dst, in_sem.at[n])
        loads[name].start()

    copies = {}

    def send(name, src, dst, device):
        n = len(copies)
        assert n < N_SEM
        copy = pltpu.make_async_remote_copy(
            src_ref=src, dst_ref=dst, send_sem=send_sem.at[n], recv_sem=recv_sem.at[n],
            device_id=device, device_id_type=MESH,
        )
        copy.start()
        copies[name] = copy

    def got(*name):
        copies[name].wait_recv()

    keys = keys_ref[...]
    loads["x"].wait()
    loads["c"].wait()
    rows_in, rows_grad = [], []
    for i in range(2):
        exponent = jnp.exp(dot_nt(keys, patches[i]))
        dispatch = exponent / jnp.sum(exponent, axis=1, keepdims=True)
        combine = exponent / (jnp.sum(exponent, axis=0, keepdims=True) + jnp.exp(ols_ref[i]))
        disp_s[i] = dispatch
        comb_s[i] = combine
        rows_in.append(dot(dispatch.astype(BF), patches[i]).astype(BF))
        rows_grad.append(dot(combine.astype(BF), cot[i]).astype(BF))
    rows = jnp.concatenate(rows_in + rows_grad, axis=0)

    def to_pieces(rows, index_of, dst):
        half = D // 2
        pieces = dot(one_hot(index_of, 0, True), rows[:, :half]) + dot(
            one_hot(index_of, 1, True), rows[:, half:]
        )
        dst[...] = pieces.astype(BF).reshape(16, 16, half)

    def from_pieces(src, index_of, half):
        pieces = src[...].reshape(256, D // 2)
        return dot(one_hot(index_of, half, False), pieces).astype(BF)

    spread = functools.partial(spread_index, me=me)
    to_pieces(rows, spread, a2s)
    a2r[0] = a2s[0]
    pl.semaphore_wait(barrier, 30)
    for off in range(1, 16):
        send(("a", off), a2s.at[off], a2r.at[off], expert_peer(off))
    for off in range(1, 16):
        got("a", off)
    for half in range(2):
        cols = slice(half * 640, half * 640 + 640)
        g[:, 0, 0, :, cols] = from_pieces(a2r, block_index, half).reshape(4, 32, 640)

    def at(ref, part, k, a1, a2, r0=0, nr=32):
        c0, nc = COLS[part]
        dy, dz = (a2, a1) if part == 0 else (a1, a2)
        return ref.at[pl.ds(2 * k, 2), dy, dz, pl.ds(r0, nr), pl.ds(c0, nc)]

    AXES = (("z", "y"), ("y", "z"))

    def ag1(part, k):
        axis = AXES[part][0]
        for step, a in ((1, 3), (-1, 1)):
            send(("p1", part, k, step), at(g, part, k, 0, 0), at(g, part, k, a, 0), ring_peer(axis, step))

    def ag1_relay(part, k):
        axis = AXES[part][0]
        for step, a, r in ((1, 3, 0), (-1, 1, 16)):
            got("p1", part, k, step)
            send(("r1", part, k, step), at(g, part, k, a, 0, r, 16), at(g, part, k, 2, 0, r, 16), ring_peer(axis, step))

    def ag1_done(part, k):
        got("r1", part, k, 1)
        got("r1", part, k, -1)

    def ag2(part, k, a1):
        axis = AXES[part][1]
        for step, a in ((1, 3), (-1, 1)):
            send(("p2", part, k, a1, step), at(g, part, k, a1, 0), at(g, part, k, a1, a), ring_peer(axis, step))

    def ag2_relay(part, k, a1):
        axis = AXES[part][1]
        for step, a, r in ((1, 3, 0), (-1, 1, 16)):
            got("p2", part, k, a1, step)
            send(("r2", part, k, a1, step), at(g, part, k, a1, a, r, 16), at(g, part, k, a1, 2, r, 16), ring_peer(axis, step))

    def ag2_done(part, k, a1):
        got("r2", part, k, a1, 1)
        got("r2", part, k, a1, -1)

    def expert(k, dy):
        x0 = g[2 * k, dy].reshape(128, D)
        x1 = g[2 * k + 1, dy].reshape(128, D)
        hidden = dot(x0, win[k])
        upstream = dot_nt(x1, wout[k])
        square = hidden * hidden
        tanh = jnp.tanh(GELU_C * (hidden + GELU_A * square * hidden))
        act = (0.5 * hidden * (1.0 + tanh)).astype(BF)
        slope = 0.5 * (1.0 + tanh) + (0.5 * hidden) * (1.0 - tanh * tanh) * (
            GELU_C + (3.0 * GELU_C * GELU_A) * square
        )
        pre = (slope * upstream).astype(BF)
        act_s[k, dy * 128 : dy * 128 + 128, :] = act
        pre_s[k, dy * 128 : dy * 128 + 128, :] = pre
        pt[2 * k, dy] = dot(act, wout[k]).astype(BF).reshape(4, 32, D)
        pt[2 * k + 1, dy] = dot_nt(pre, win[k]).astype(BF).reshape(4, 32, D)

    def weight_grads(k):
        wog[k] = dot_tn(act_s[k], g[2 * k + 1].reshape(512, D)).astype(BF)
        wig[k] = dot_tn(g[2 * k].reshape(512, D), pre_s[k]).astype(BF)
        for n, (src, dst) in enumerate(((wig, wig_hbm), (wog, wog_hbm))):
            stores.append(pltpu.make_async_copy(src.at[k], dst.at[k], out_sem.at[2 * k + n]))
            stores[-1].start()

    stores = []

    UP, TP, MP, UM, TM, MM = range(6)

    def wide(ref, part, k, a2, r0):
        c0, nc = COLS[part]
        if part == 0:
            return ref.at[pl.ds(2 * k, 2), a2, :, pl.ds(r0, 16), pl.ds(c0, nc)]
        return ref.at[pl.ds(2 * k, 2), :, a2, pl.ds(r0, 16), pl.ds(c0, nc)]

    def land(ph, part, k, m):
        c0, nc = COLS[part]
        if ph == 1:
            return r1.at[k, m, :, :, :, pl.ds(c0, nc)]
        return r2.at[k, m, :, :, pl.ds(c0, nc)]

    def part_of(ph, part, k, a, r0):
        if ph == 1:
            return wide(pt, part, k, a, r0)
        return at(pt, part, k, a, 0, r0, 16)

    def rs_send(ph, part, k, m, a, r0):
        axis = AXES[part][2 - ph]
        step = 1 if m < 3 else -1
        send(("rs", ph, part, k, m), part_of(ph, part, k, a, r0), land(ph, part, k, m), ring_peer(axis, step))

    def rs_u(ph, part, k):
        rs_send(ph, part, k, UP, 1, 0)
        rs_send(ph, part, k, UM, 3, 16)

    def rs_t(ph, part, k):
        rs_send(ph, part, k, TP, 2, 16)
        rs_send(ph, part, k, TM, 2, 0)

    def add_into(dst, *srcs):
        total = dst[...].astype(F32)
        for src in srcs:
            total = total + src[...].astype(F32)
        dst[...] = total.astype(BF)

    def rs_m(ph, part, k):
        for t, m, a, r0 in ((TP, MP, 1, 16), (TM, MM, 3, 0)):
            got("rs", ph, part, k, t)
            add_into(part_of(ph, part, k, a, r0), land(ph, part, k, t))
            rs_send(ph, part, k, m, a, r0)

    def rs_final(ph, part, k):
        for u, m, r0 in ((UP, MM, 0), (UM, MP, 16)):
            got("rs", ph, part, k, u)
            got("rs", ph, part, k, m)
            add_into(part_of(ph, part, k, 0, r0), land(ph, part, k, u), land(ph, part, k, m))

    A, B = 0, 1
    ag1(A, 0)
    ag1(B, 0)
    ag2(A, 0, 0)
    ag2(B, 0, 0)
    ag1_relay(B, 0)
    ag2(B, 0, 3)
    ag2(B, 0, 1)
    ag2(A, 1, 0)
    ag2_relay(A, 0, 0)
    ag1_relay(A, 0)
    ag2(A, 0, 3)
    ag2(A, 0, 1)
    ag1(A, 1)
    ag1(B, 1)
    ag2_relay(A, 1, 0)
    ag1_done(B, 0)
    ag2(B, 0, 2)
    ag2_relay(B, 0, 0)
    ag2_relay(B, 0, 3)
    ag2_relay(B, 0, 1)
    ag1_done(A, 0)
    ag2(A, 0, 2)
    ag2_relay(A, 0, 3)
    ag2_relay(A, 0, 1)
    ag2_relay(B, 0, 2)
    ag1_relay(B, 1)
    ag2(B, 1, 0)
    ag2(B, 1, 3)
    ag2(B, 1, 1)
    ag2_done(B, 0, 0)
    loads["wi"].wait()
    loads["wo"].wait()
    expert(0, 0)
    ag2_relay(A, 0, 2)
    ag1_relay(A, 1)
    ag2(A, 1, 3)
    ag2(A, 1, 1)
    ag1_done(B, 1)
    ag2(B, 1, 2)
    ag2_done(B, 0, 3)
    expert(0, 3)
    ag2_relay(B, 1, 0)
    ag2_relay(B, 1, 3)
    ag2_relay(B, 1, 1)
    ag1_done(A, 1)
    ag2(A, 1, 2)
    ag2_done(B, 0, 1)
    expert(0, 1)
    ag2_relay(A, 1, 3)
    ag2_relay(A, 1, 1)
    ag2_relay(B, 1, 2)
    for a in (0, 3, 1, 2):
        ag2_done(A, 0, a)
    ag2_done(B, 0, 2)
    rs_u(1, A, 0)
    expert(0, 2)
    rs_t(1, A, 0)
    rs_t(1, B, 0)
    rs_u(1, B, 0)
    ag2_relay(A, 1, 2)
    ag2_done(B, 1, 0)
    expert(1, 0)
    rs_m(1, A, 0)
    rs_m(1, B, 0)
    ag2_done(B, 1, 3)
    expert(1, 3)
    ag2_done(B, 1, 1)
    expert(1, 1)
    rs_u(1, A, 1)
    for a in (0, 3, 1, 2):
        ag2_done(A, 1, a)
    ag2_done(B, 1, 2)
    expert(1, 2)
    rs_t(1, A, 1)
    rs_t(1, B, 1)
    rs_u(1, B, 1)
    for part in (B, A):
        rs_final(1, part, 0)
        rs_t(2, part, 0)
        rs_u(2, part, 0)
    rs_m(1, A, 1)
    rs_m(1, B, 1)
    weight_grads(0)
    rs_m(2, B, 0)
    rs_m(2, A, 0)
    weight_grads(1)
    for part in (B, A):
        rs_final(1, part, 1)
        rs_t(2, part, 1)
        rs_u(2, part, 1)
    rs_final(2, B, 0)
    rs_final(2, A, 0)
    rs_m(2, B, 1)
    rs_m(2, A, 1)
    rs_final(2, B, 1)
    rs_final(2, A, 1)

    to_pieces(pt[:, 0, 0].reshape(128, D), block_index, b2s)
    b2r[0] = b2s[0]
    for off in range(1, 16):
        send(("b", off), b2s.at[off], b2r.at[off], expert_peer(16 - off))
    for off in range(1, 16):
        got("b", off)
    back = jnp.concatenate([from_pieces(b2r, spread, half) for half in range(2)], axis=1)

    halves = []
    key_part = jnp.zeros((32, D), F32)
    for i in range(2):
        slot_out = back[i * 32 : i * 32 + 32]
        slot_in_grad = back[64 + i * 32 : 96 + i * 32]
        comb_grad = dot_nt(slot_out, cot[i])
        disp_grad = dot_nt(slot_in_grad, patches[i])
        dispatch = disp_s[i]
        combine = comb_s[i]
        logit_grad = combine * (comb_grad - jnp.sum(combine * comb_grad, axis=0, keepdims=True))
        logit_grad = logit_grad + dispatch * (
            disp_grad - jnp.sum(dispatch * disp_grad, axis=1, keepdims=True)
        )
        logit_half = logit_grad.astype(BF)
        key_part = key_part + dot(logit_half, patches[i])
        halves.append((dispatch.astype(BF), logit_half, slot_in_grad))

    for o in range(16):
        rg, c0 = o // 4, (o % 4) * 384
        nc = min(384, D - c0)
        ks[o, :, :nc] = key_part[rg * 8 : rg * 8 + 8, c0 : c0 + nc]
        if nc < 384:
            ks[o, :, nc:] = jnp.zeros((8, 384 - nc), F32)
    for off in range(1, 16):
        send(("k1", off), ks.at[lax.rem(me + off, 16)], k1.at[off], expert_peer(off))

    def image_out(i):
        dispatch_half, logit_half, slot_in_grad = halves[i]
        lhs = jnp.concatenate([dispatch_half, logit_half], axis=0)
        rhs = jnp.concatenate([slot_in_grad, keys], axis=0)
        pg[i] = dot_tn(lhs, rhs).astype(BF)
        stores.append(pltpu.make_async_copy(pg.at[i], pg_hbm.at[i], out_sem.at[4 + i]))
        stores[-1].start()

    image_out(0)
    total = ks[me]
    for off in range(1, 16):
        got("k1", off)
        total = total + k1[off]
    k2[0] = total
    for off in range(1, 16):
        send(("k2", off), k2.at[0], k2.at[off], dp_peer(off))
    image_out(1)
    for off in range(1, 16):
        got("k2", off)
    total = k2[lax.rem(dp, 16)]
    for n in range(1, 16):
        total = total + k2[lax.rem(dp + 16 - n, 16)]
    k3[0] = total
    for off in range(1, 16):
        send(("k3", off), k3.at[0], k3.at[off], expert_peer(off))
    k4[me] = total
    for off in range(1, 16):
        got("k3", off)
        k4[lax.rem(me + 16 - off, 16)] = k3[off]
    for o in range(16):
        rg, c0 = o // 4, (o % 4) * 384
        nc = min(384, D - c0)
        kg_ref[rg * 8 : rg * 8 + 8, c0 : c0 + nc] = k4[o, :, :nc]
    for store in stores:
        store.wait()
    for copy in copies.values():
        copy.wait_send()


def on_device(patches, cotangent, other_logsum, slot_keys, w_in, w_out):
    any_spec = pl.BlockSpec(memory_space=pl.ANY)
    vmem = pl.BlockSpec(memory_space=pltpu.VMEM)
    return pl.pallas_call(
        kernel,
        out_shape=(
            jax.ShapeDtypeStruct((2, 256, D), BF),
            jax.ShapeDtypeStruct((32, D), F32),
            jax.ShapeDtypeStruct((2, D, FB), BF),
            jax.ShapeDtypeStruct((2, FB, D), BF),
        ),
        in_specs=[any_spec, any_spec, vmem, vmem, any_spec, any_spec],
        out_specs=(any_spec, vmem, any_spec, any_spec),
        scratch_shapes=[
            pltpu.VMEM((2, 256, D), BF),
            pltpu.VMEM((2, 256, D), BF),
            pltpu.VMEM((2, D, FB), BF),
            pltpu.VMEM((2, FB, D), BF),
            pltpu.VMEM((2, 256, D), BF),
            pltpu.VMEM((2, D, FB), BF),
            pltpu.VMEM((2, FB, D), BF),
            pltpu.VMEM((2, 32, 256), F32),
            pltpu.VMEM((2, 32, 256), F32),
            pltpu.VMEM((4, 4, 4, 32, D), BF),
            pltpu.VMEM((4, 4, 4, 32, D), BF),
            pltpu.VMEM((2, 512, FB), BF),
            pltpu.VMEM((2, 512, FB), BF),
            pltpu.VMEM((2, 6, 2, 4, 16, D), BF),
            pltpu.VMEM((2, 6, 2, 16, D), BF),
            pltpu.VMEM((16, 16, D // 2), BF),
            pltpu.VMEM((16, 16, D // 2), BF),
            pltpu.VMEM((16, 16, D // 2), BF),
            pltpu.VMEM((16, 16, D // 2), BF),
            pltpu.VMEM((16, 8, 384), F32),
            pltpu.VMEM((16, 8, 384), F32),
            pltpu.VMEM((16, 8, 384), F32),
            pltpu.VMEM((16, 8, 384), F32),
            pltpu.VMEM((16, 8, 384), F32),
            pltpu.SemaphoreType.DMA((N_SEM,)),
            pltpu.SemaphoreType.DMA((N_SEM,)),
            pltpu.SemaphoreType.DMA((4,)),
            pltpu.SemaphoreType.DMA((6,)),
        ],
        compiler_params=pltpu.CompilerParams(
            collective_id=0, has_side_effects=True, vmem_limit_bytes=56 * 2**20
        ),
        name="soft_moe_backward",
    )(patches, cotangent, other_logsum[:, None, :], slot_keys, w_in, w_out)


def solution(mesh):
    placed = (
        P(("dp", "expert"), None, None),
        P(("dp", "expert"), None, None),
        P(("dp", "expert"), None),
        P(),
        P("expert", None, "dp"),
        P("expert", "dp", None),
    )
    return jax.shard_map(
        on_device,
        mesh=mesh,
        in_specs=placed,
        out_specs=(
            P(("dp", "expert"), None, None),
            P(),
            P("expert", None, "dp"),
            P("expert", "dp", None),
        ),
        check_vma=False,
    )
```

```python
import functools

import jax
import jax.numpy as jnp
from jax import lax
from jax.experimental import pallas as pl
from jax.experimental.pallas import tpu as pltpu
from jax.sharding import PartitionSpec as P

MESH = pl.DeviceIdType.MESH
BF = jnp.bfloat16
F32 = jnp.float32

D = 1280
FB = 320
SPLIT = 1024
COLS = {"A": (0, SPLIT), "B": (SPLIT, D - SPLIT)}
N_RECV = 80
N_SEND = 10
KEY_COLS = (0, 384, 768, 1024)
GELU_C = 0.7978845608028654
GELU_A = 0.044715

ORDER = (
    ("ag1", "A", 0), ("ag1", "B", 0), ("ag2", "A", 1, 0), ("ag2", "A", 0, 0), ("ag2", "B", 0, 0), ("ag1", "B", 1),
    ("ag1", "A", 1), ("ag1_relay", "B", 0), ("ag2_relay", "A", 1, 0), ("ag2", "B", 0, 3), ("ag2_relay", "A", 0, 0),
    ("ag1_relay", "B", 1), ("ag1_relay", "A", 0), ("ag2", "A", 0, 1), ("ag2", "A", 0, 3), ("ag2_relay", "B", 0, 0),
    ("ag2", "B", 0, 1), ("ag2", "B", 0, 2), ("ag2", "B", 1, 1), ("ag2_relay", "A", 0, 1), ("ag2_relay", "B", 0, 3),
    ("ag2", "B", 1, 0), ("ag2_relay", "A", 0, 3), ("ag1_relay", "A", 1), ("ag2", "A", 0, 2), ("ag2", "A", 1, 1),
    ("expert", 0, 0), ("ag2_relay", "B", 0, 1), ("ag2", "A", 1, 3), ("ag2", "B", 1, 2), ("ag2_relay", "B", 0, 2),
    ("ag2_relay", "B", 1, 1), ("ag2_relay", "A", 0, 2), ("expert", 0, 3), ("ag2_relay", "B", 1, 0),
    ("ag2", "B", 1, 3), ("ag2_relay", "A", 1, 1), ("ag2", "A", 1, 2), ("expert", 0, 1), ("rs1_u", "A", 0, 1),
    ("ag2_relay", "B", 1, 2), ("rs1_u", "A", 0, 0), ("ag2_relay", "A", 1, 3), ("expert", 0, 2),
    ("rs1_t", "A", 0, 2), ("ag2_relay", "B", 1, 3), ("rs1_t", "A", 0, 1), ("rs1_t", "B", 0), ("rs1_u", "B", 0),
    ("expert", 1, 0), ("ag2_relay", "A", 1, 2), ("expert", 1, 1), ("rs1_u", "A", 0, 2), ("rs1_t", "A", 0, 3),
    ("expert", 1, 3), ("rs1_m", "B", 0), ("rs1_m", "A", 0, 1), ("rs1_m", "A", 0, 2), ("expert", 1, 2),
    ("rs1_t", "B", 1), ("rs1_t", "A", 1, 2), ("rs1_m", "A", 0, 3), ("rs1_f", "A", 0, 1), ("rs1_u", "B", 1),
    ("rs1_t", "A", 1, 1), ("rs1_u", "A", 0, 3), ("rs1_t", "A", 1, 3), ("rs1_f", "B", 0), ("rs1_f", "A", 0, 2),
    ("rs2_u", "B", 0), ("rs2_t", "A", 0), ("rs1_u", "A", 1, 3), ("weight_grads", 0), ("rs1_m", "B", 1),
    ("rs1_m", "A", 1, 2), ("rs1_m", "A", 1, 1), ("rs1_u", "A", 1, 2), ("rs1_u", "A", 1, 1), ("rs1_f", "A", 0, 3),
    ("rs2_u", "A", 0), ("weight_grads", 1), ("rs2_m", "A", 0), ("rs1_m", "A", 1, 3), ("rs1_f", "B", 1),
    ("rs2_t", "B", 1), ("rs2_u", "B", 1), ("rs1_t", "A", 1, 0), ("rs2_t", "B", 0), ("rs1_f", "A", 1, 2),
    ("rs1_u", "A", 1, 0), ("rs2_t", "A", 1), ("rs1_t", "A", 0, 0), ("rs1_f", "A", 1, 1), ("rs1_f", "A", 1, 3),
    ("rs2_m", "B", 1), ("rs2_u", "A", 1), ("rs1_m", "A", 1, 0), ("rs2_m", "B", 0), ("rs2_m", "A", 1),
    ("rs1_m", "A", 0, 0), ("rs2_f", "B", 1), ("rs1_f", "A", 1, 0), ("rs2_f", "B", 0), ("rs1_f", "A", 0, 0),
    ("rs2_f", "A", 0), ("rs2_f", "A", 1),
)


def dot(a, b):
    return lax.dot_general(a, b, (((1,), (0,)), ((), ())), preferred_element_type=F32)


def dot_nt(a, b):
    return lax.dot_general(a, b, (((1,), (1,)), ((), ())), preferred_element_type=F32)


def dot_tn(a, b):
    return lax.dot_general(a, b, (((0,), (0,)), ((), ())), preferred_element_type=F32)


def iota(shape, dim):
    return lax.broadcasted_iota(jnp.int32, shape, dim)


def piece_row(slot_off, half, k, t, i):
    return slot_off * 16 + half * 8 + k * 4 + t * 2 + i


def spread_index(r, me):
    off, k, t, i = r >> 4, (r >> 2) & 1, (r >> 1) & 1, r & 1
    owner = (me + off) & 15
    return (t * 2 + i) * 32 + 2 * owner + k


def block_index(r):
    off, k, t, i = r >> 4, (r >> 2) & 1, (r >> 1) & 1, r & 1
    return (k * 2 + t) * 32 + off * 2 + i


def one_hot(index_of, half, rows_are_pieces):
    shape = (256, 128) if rows_are_pieces else (128, 256)
    piece = iota(shape, 0 if rows_are_pieces else 1)
    other = iota(shape, 1 if rows_are_pieces else 0)
    hit = (index_of(piece) == other) & (((piece >> 3) & 1) == half)
    return jnp.where(hit, 1.0, 0.0).astype(BF)


def kernel(
    patches_hbm, cot_hbm, ols_ref, keys_ref, win_hbm, wout_hbm,
    pg_hbm, kg_ref, wig_hbm, wog_hbm,
    patches, cot, win, wout, pg, wig, wog,
    disp_s, comb_s, g, pt, act_s, pre_s, r1, r2,
    a2s, a2r, b2s, b2r, ks, k1, k2, k3, k4,
    send_sem, recv_sem, in_sem, out_sem,
):
    dp = lax.axis_index("dp")
    me = lax.axis_index("expert")
    zh, y = dp // 4, dp % 4

    def expert_peer(off):
        return (dp, lax.rem(me + off, 16))

    def dp_peer(off):
        return (lax.rem(dp + off, 16), me)

    def ring_peer(axis, step):
        if axis == "y":
            return (zh * 4 + lax.rem(y + step + 4, 4), me)
        return (lax.rem(zh + step + 4, 4) * 4 + y, me)

    barrier = pltpu.get_barrier_semaphore()
    for off in range(1, 16):
        pl.semaphore_signal(barrier, inc=1, device_id=expert_peer(off), device_id_type=MESH)
        pl.semaphore_signal(barrier, inc=1, device_id=dp_peer(off), device_id_type=MESH)

    loads = {}
    for n, (name, src, dst) in enumerate(
        (("x", patches_hbm, patches), ("c", cot_hbm, cot), ("wi", win_hbm, win), ("wo", wout_hbm, wout))
    ):
        loads[name] = pltpu.make_async_copy(src, dst, in_sem.at[n])
    loads["x"].start()
    loads["c"].start()

    recv_of, send_of, waited = {}, {}, set()

    def send(group, out, src, dst, device):
        n = recv_of.setdefault(group, len(recv_of))
        m = send_of.setdefault(out, len(send_of))
        assert n < N_RECV and m < N_SEND
        pltpu.make_async_remote_copy(
            src_ref=src, dst_ref=dst, send_sem=send_sem.at[m], recv_sem=recv_sem.at[n],
            device_id=device, device_id_type=MESH,
        ).start()

    def total_of(ref, n, m):
        return pltpu.make_async_remote_copy(
            src_ref=ref, dst_ref=ref, send_sem=send_sem.at[m], recv_sem=recv_sem.at[n],
            device_id=expert_peer(1), device_id_type=MESH,
        )

    def got(group, ref):
        if group not in waited:
            waited.add(group)
            total_of(ref, recv_of[group], 0).wait_recv()

    def sent(out, ref):
        total_of(ref, 0, send_of.pop(out)).wait_send()

    keys = keys_ref[...]
    loads["x"].wait()
    loads["c"].wait()
    loads["wi"].start()
    loads["wo"].start()
    rows_in, rows_grad = [], []
    for i in range(2):
        exponent = jnp.exp(dot_nt(keys, patches[i]))
        dispatch = exponent / jnp.sum(exponent, axis=1, keepdims=True)
        combine = exponent / (jnp.sum(exponent, axis=0, keepdims=True) + jnp.exp(ols_ref[i : i + 1, :]))
        disp_s[i] = dispatch
        comb_s[i] = combine
        rows_in.append(dot(dispatch.astype(BF), patches[i]).astype(BF))
        rows_grad.append(dot(combine.astype(BF), cot[i]).astype(BF))
    rows = jnp.concatenate(rows_in + rows_grad, axis=0)

    def to_pieces(rows, index_of, dst):
        half = D // 2
        pieces = dot(one_hot(index_of, 0, True), rows[:, :half]) + dot(
            one_hot(index_of, 1, True), rows[:, half:]
        )
        dst[...] = pieces.astype(BF).reshape(16, 16, half)

    def from_pieces(src, index_of, half):
        pieces = src[...].reshape(256, D // 2)
        return dot(one_hot(index_of, half, False), pieces).astype(BF)

    spread = functools.partial(spread_index, me=me)
    to_pieces(rows, spread, a2s)
    a2r[0] = a2s[0]
    pl.semaphore_wait(barrier, 30)
    for off in range(1, 16):
        send("a", "a", a2s.at[off], a2r.at[off], expert_peer(off))
    got("a", a2r.at[pl.ds(1, 15)])
    for half in range(2):
        cols = slice(half * 640, half * 640 + 640)
        g[:, 0, 0, :, cols] = from_pieces(a2r, block_index, half).reshape(4, 32, 640)

    AXES = {"A": ("z", "y"), "B": ("y", "z")}

    def cols_of(part):
        return pl.ds(*COLS[part])

    def at(ref, part, k, a1, a2, r0=0, nr=32):
        dy, dz = (a2, a1) if part == "A" else (a1, a2)
        return ref.at[pl.ds(2 * k, 2), dy, dz, pl.ds(r0, nr), cols_of(part)]

    def two(part, k):
        return g.at[pl.ds(2 * k, 2), 0, pl.ds(0, 2), :, cols_of(part)]

    def ag1(part, k):
        for step, a in ((1, 3), (-1, 1)):
            send(("p1", part, k), "ag1", at(g, part, k, 0, 0), at(g, part, k, a, 0), ring_peer(AXES[part][0], step))

    def ag1_relay(part, k):
        got(("p1", part, k), two(part, k))
        for step, a, r in ((1, 3, 0), (-1, 1, 16)):
            send(("r1", part, k), "ag1", at(g, part, k, a, 0, r, 16), at(g, part, k, 2, 0, r, 16), ring_peer(AXES[part][0], step))

    def first_in(part, k, a1):
        if a1 in (1, 3):
            got(("p1", part, k), two(part, k))
        if a1 == 2:
            got(("r1", part, k), at(g, part, k, 2, 0))

    def ag2(part, k, a1):
        first_in(part, k, a1)
        for step, a in ((1, 3), (-1, 1)):
            send(("p2", part, k, a1), "ag2", at(g, part, k, a1, 0), at(g, part, k, a1, a), ring_peer(AXES[part][1], step))

    def ag2_relay(part, k, a1):
        got(("p2", part, k, a1), two(part, k))
        for step, a, r in ((1, 3, 0), (-1, 1, 16)):
            send(("r2", part, k, a1), "ag2", at(g, part, k, a1, a, r, 16), at(g, part, k, a1, 2, r, 16), ring_peer(AXES[part][1], step))

    def slot_in(part, k, a1, a2):
        if a2 == 0:
            first_in(part, k, a1)
        elif a2 == 2:
            got(("r2", part, k, a1), at(g, part, k, a1, 2))
        else:
            got(("p2", part, k, a1), two(part, k))

    def expert(k, dy):
        for n in range(4):
            slot_in("A", k, n, dy)
            slot_in("B", k, dy, n)
        if "w" not in waited:
            waited.add("w")
            loads["wi"].wait()
            loads["wo"].wait()
        x0 = g[2 * k, dy].reshape(128, D)
        x1 = g[2 * k + 1, dy].reshape(128, D)
        hidden = dot_nt(x0, win[k])
        upstream = dot_nt(x1, wout[k])
        square = hidden * hidden
        tanh = jnp.tanh(GELU_C * (hidden + GELU_A * square * hidden))
        act = (0.5 * hidden * (1.0 + tanh)).astype(BF)
        slope = 0.5 * (1.0 + tanh) + (0.5 * hidden) * (1.0 - tanh * tanh) * (
            GELU_C + (3.0 * GELU_C * GELU_A) * square
        )
        pre = (slope * upstream).astype(BF)
        act_s[k, dy * 128 : dy * 128 + 128, :] = act
        pre_s[k, dy * 128 : dy * 128 + 128, :] = pre
        pt[2 * k, dy] = dot(act, wout[k]).astype(BF).reshape(4, 32, D)
        pt[2 * k + 1, dy] = dot(pre, win[k]).astype(BF).reshape(4, 32, D)

    def weight_grads(k):
        wog[k] = dot_tn(act_s[k], g[2 * k + 1].reshape(512, D)).astype(BF)
        wig[k] = dot_tn(pre_s[k], g[2 * k].reshape(512, D)).astype(BF)
        for n, (src, dst) in enumerate(((wig, wig_hbm), (wog, wog_hbm))):
            stores.append(pltpu.make_async_copy(src.at[k], dst.at[k], out_sem.at[2 * k + n]))
            stores[-1].start()

    stores = []

    TP, TM, UP, MP, UM, MM = range(6)

    def part_of(ph, part, k, a1, a2, r0):
        if ph == 1 and part == "B":
            return pt.at[pl.ds(2 * k, 2), :, a2, pl.ds(r0, 16), cols_of(part)]
        if ph == 1:
            return at(pt, part, k, a1, a2, r0, 16)
        return at(pt, part, k, a2, 0, r0, 16)

    def land(ph, part, k, a1, m):
        if ph == 1:
            return r1.at[k, m, :, slice(None) if part == "B" else a1, :, cols_of(part)]
        return r2.at[k, m, :, :, cols_of(part)]

    def rs_send(ph, part, k, a1, m, a2, r0):
        step = 1 if m in (TP, UP, MP) else -1
        kind = "t" if m < 2 else "u"
        send((kind, ph, part, k, a1), ("rs", ph), part_of(ph, part, k, a1, a2, r0), land(ph, part, k, a1, m), ring_peer(AXES[part][2 - ph], step))

    def rs_got(ph, part, k, a1, kind):
        m = pl.ds(0, 2) if kind == "t" else pl.ds(2, 4)
        got((kind, ph, part, k, a1), land(ph, part, k, a1, m))

    def rs_t(ph, part, k, a1=None):
        rs_send(ph, part, k, a1, TP, 2, 16)
        rs_send(ph, part, k, a1, TM, 2, 0)

    def rs_u(ph, part, k, a1=None):
        rs_send(ph, part, k, a1, UP, 1, 0)
        rs_send(ph, part, k, a1, UM, 3, 16)

    def add_into(dst, *srcs):
        total = dst[...].astype(F32)
        for src in srcs:
            total = total + src[...].astype(F32)
        dst[...] = total.astype(BF)

    def rs_m(ph, part, k, a1=None):
        rs_got(ph, part, k, a1, "t")
        for t, m, a2, r0 in ((TP, MP, 1, 16), (TM, MM, 3, 0)):
            add_into(part_of(ph, part, k, a1, a2, r0), land(ph, part, k, a1, t))
            rs_send(ph, part, k, a1, m, a2, r0)

    def rs_f(ph, part, k, a1=None):
        rs_got(ph, part, k, a1, "u")
        for u, m, r0 in ((UP, MM, 0), (UM, MP, 16)):
            add_into(part_of(ph, part, k, a1, 0, r0), land(ph, part, k, a1, u), land(ph, part, k, a1, m))

    steps = {"ag1": ag1, "ag1_relay": ag1_relay, "ag2": ag2, "ag2_relay": ag2_relay, "expert": expert, "weight_grads": weight_grads}
    for ph in (1, 2):
        for name, step in (("t", rs_t), ("u", rs_u), ("m", rs_m), ("f", rs_f)):
            steps["rs%d_%s" % (ph, name)] = functools.partial(step, ph)
    for name, *where in ORDER:
        steps[name](*where)

    to_pieces(pt[:, 0, 0].reshape(128, D), block_index, b2s)
    b2r[0] = b2s[0]
    for off in range(1, 16):
        send("b", "b", b2s.at[off], b2r.at[off], expert_peer(16 - off))
    got("b", b2r.at[pl.ds(1, 15)])
    back = jnp.concatenate([from_pieces(b2r, spread, half) for half in range(2)], axis=1)

    halves = []
    key_part = jnp.zeros((32, D), F32)
    for i in range(2):
        slot_out = back[i * 32 : i * 32 + 32]
        slot_in_grad = back[64 + i * 32 : 96 + i * 32]
        comb_grad = dot_nt(slot_out, cot[i])
        disp_grad = dot_nt(slot_in_grad, patches[i])
        dispatch = disp_s[i]
        combine = comb_s[i]
        logit_grad = combine * (comb_grad - jnp.sum(combine * comb_grad, axis=0, keepdims=True))
        logit_grad = logit_grad + dispatch * (
            disp_grad - jnp.sum(dispatch * disp_grad, axis=1, keepdims=True)
        )
        logit_half = logit_grad.astype(BF)
        key_part = key_part + dot(logit_half, patches[i])
        halves.append((dispatch.astype(BF), logit_half, slot_in_grad))

    for o in range(16):
        rg, c0 = (o // 4) * 8, KEY_COLS[o % 4]
        top = key_part[rg : rg + 8, c0 : c0 + 256]
        low = jnp.zeros((8, 256), F32)
        if o % 4 < 2:
            low = jnp.concatenate([key_part[rg : rg + 8, c0 + 256 : c0 + 384], low[:, :128]], axis=1)
        ks[o] = jnp.concatenate([top, low], axis=0).astype(BF)
    for off in range(1, 16):
        send("k1", "k1", ks.at[lax.rem(me + off, 16)], k1.at[off], expert_peer(off))

    def image_out(i):
        dispatch_half, logit_half, slot_in_grad = halves[i]
        lhs = jnp.concatenate([dispatch_half, logit_half], axis=0)
        rhs = jnp.concatenate([slot_in_grad, keys], axis=0)
        pg[i] = dot_tn(lhs, rhs).astype(BF)
        stores.append(pltpu.make_async_copy(pg.at[i], pg_hbm.at[i], out_sem.at[4 + i]))
        stores[-1].start()

    image_out(0)
    total = ks[me].astype(F32)
    got("k1", k1.at[pl.ds(1, 15)])
    for off in range(1, 16):
        total = total + k1[off].astype(F32)
    k2[0] = total.astype(BF)
    for off in range(1, 16):
        send("k2", "k2", k2.at[0], k2.at[off], dp_peer(off))
    image_out(1)
    got("k2", k2.at[pl.ds(1, 15)])
    total = k2[lax.rem(dp, 16)].astype(F32)
    for n in range(1, 16):
        total = total + k2[lax.rem(dp + 16 - n, 16)].astype(F32)
    k3[0] = total.astype(BF)
    for off in range(1, 16):
        send("k3", "k3", k3.at[0], k3.at[off], expert_peer(off))
    k4[me] = k3[0]
    got("k3", k3.at[pl.ds(1, 15)])
    for off in range(1, 16):
        k4[lax.rem(me + 16 - off, 16)] = k3[off]
    for o in range(16):
        rg, c0 = (o // 4) * 8, KEY_COLS[o % 4]
        piece = k4[o].astype(F32)
        kg_ref[rg : rg + 8, c0 : c0 + 256] = piece[:8]
        if o % 4 < 2:
            kg_ref[rg : rg + 8, c0 + 256 : c0 + 384] = piece[8:, :128]
    for store in stores:
        store.wait()
    for out, ref in (("a", a2s), ("b", b2s), ("k1", k1), ("k2", k2), ("k3", k3)):
        sent(out, ref.at[pl.ds(1, 15)])
    sent("ag1", g.at[:, 0, pl.ds(1, 3)])
    sent("ag2", g.at[:, pl.ds(1, 3)])
    sent(("rs", 1), r1)
    sent(("rs", 2), r2)
    assert not send_of and len(waited) == len(recv_of) + 1


def on_device(patches, cotangent, other_logsum, slot_keys, w_in, w_out):
    any_spec = pl.BlockSpec(memory_space=pl.ANY)
    vmem = pl.BlockSpec(memory_space=pltpu.VMEM)
    patch_grad, key_grad, w_in_grad, w_out_grad = pl.pallas_call(
        kernel,
        out_shape=(
            jax.ShapeDtypeStruct((2, 256, D), BF),
            jax.ShapeDtypeStruct((32, D), F32),
            jax.ShapeDtypeStruct((2, FB, D), BF),
            jax.ShapeDtypeStruct((2, FB, D), BF),
        ),
        in_specs=[any_spec, any_spec, vmem, vmem, any_spec, any_spec],
        out_specs=(any_spec, vmem, any_spec, any_spec),
        scratch_shapes=[
            pltpu.VMEM((2, 256, D), BF),
            pltpu.VMEM((2, 256, D), BF),
            pltpu.VMEM((2, FB, D), BF),
            pltpu.VMEM((2, FB, D), BF),
            pltpu.VMEM((2, 256, D), BF),
            pltpu.VMEM((2, FB, D), BF),
            pltpu.VMEM((2, FB, D), BF),
            pltpu.VMEM((2, 32, 256), F32),
            pltpu.VMEM((2, 32, 256), F32),
            pltpu.VMEM((4, 4, 4, 32, D), BF),
            pltpu.VMEM((4, 4, 4, 32, D), BF),
            pltpu.VMEM((2, 512, FB), BF),
            pltpu.VMEM((2, 512, FB), BF),
            pltpu.VMEM((2, 6, 2, 4, 16, D), BF),
            pltpu.VMEM((2, 6, 2, 16, D), BF),
            pltpu.VMEM((16, 16, D // 2), BF),
            pltpu.VMEM((16, 16, D // 2), BF),
            pltpu.VMEM((16, 16, D // 2), BF),
            pltpu.VMEM((16, 16, D // 2), BF),
            pltpu.VMEM((16, 16, 256), BF),
            pltpu.VMEM((16, 16, 256), BF),
            pltpu.VMEM((16, 16, 256), BF),
            pltpu.VMEM((16, 16, 256), BF),
            pltpu.VMEM((16, 16, 256), BF),
            pltpu.SemaphoreType.DMA((N_SEND,)),
            pltpu.SemaphoreType.DMA((N_RECV,)),
            pltpu.SemaphoreType.DMA((4,)),
            pltpu.SemaphoreType.DMA((6,)),
        ],
        compiler_params=pltpu.CompilerParams(
            collective_id=0, has_side_effects=True, vmem_limit_bytes=56 * 2**20
        ),
        name="soft_moe_backward",
    )(patches, cotangent, other_logsum, slot_keys, jnp.swapaxes(w_in, 1, 2), w_out)
    return (patch_grad, key_grad, jnp.swapaxes(w_in_grad, 1, 2), w_out_grad)


def solution(mesh):
    placed = (
        P(("dp", "expert"), None, None),
        P(("dp", "expert"), None, None),
        P(("dp", "expert"), None),
        P(),
        P("expert", None, "dp"),
        P("expert", "dp", None),
    )
    return jax.shard_map(
        on_device,
        mesh=mesh,
        in_specs=placed,
        out_specs=(
            P(("dp", "expert"), None, None),
            P(),
            P("expert", None, "dp"),
            P("expert", "dp", None),
        ),
        check_vma=False,
    )
```

```python
import functools

import jax
import jax.numpy as jnp
from jax import lax
from jax.experimental import pallas as pl
from jax.experimental.pallas import tpu as pltpu
from jax.sharding import PartitionSpec as P

MESH = pl.DeviceIdType.MESH
BF = jnp.bfloat16
F32 = jnp.float32

D = 1280
FB = 320
SPLIT = 1024
COLS = {"A": (0, SPLIT), "B": (SPLIT, D - SPLIT)}
N_RECV = 80
N_SEND = 10
OWNERS = 10
GELU_C = 0.7978845608028654
GELU_A = 0.044715

ORDER = (
    ("ag2", "A", 1, 0), ("ag1", "B", 0), ("ag1", "A", 0), ("ag2", "B", 0, 0), ("ag2", "A", 0, 0), ("ag1", "B", 1),
    ("ag1", "A", 1), ("ag2_relay", "A", 1, 0), ("ag1_relay", "B", 0), ("ag2", "B", 0, 1), ("ag2_relay", "A", 0, 0),
    ("ag2", "B", 0, 3), ("ag1_relay", "B", 1), ("ag1_relay", "A", 0), ("ag2", "A", 0, 1), ("ag2", "A", 0, 3),
    ("ag2_relay", "B", 0, 0), ("ag2", "B", 1, 3), ("ag2", "B", 1, 0), ("ag2_relay", "A", 0, 1),
    ("ag1_relay", "A", 1), ("ag2", "A", 1, 1), ("ag2", "A", 1, 3), ("ag2_relay", "A", 0, 3),
    ("ag2_relay", "B", 0, 3), ("ag2_relay", "B", 0, 1), ("ag2", "B", 0, 2), ("ag2", "A", 0, 2), ("ag2", "B", 1, 2),
    ("expert", 0, 0), ("ag2_relay", "A", 1, 1), ("ag2_relay", "B", 1, 3), ("ag2", "B", 1, 1),
    ("ag2_relay", "A", 1, 3), ("ag2_relay", "B", 1, 0), ("ag2", "A", 1, 2), ("ag2_relay", "A", 0, 2),
    ("expert", 0, 1), ("ag2_relay", "B", 0, 2), ("expert", 0, 3), ("rs1_u", "A", 0, 1), ("rs1_u", "A", 0, 2),
    ("ag2_relay", "B", 1, 1), ("ag2_relay", "B", 1, 2), ("rs1_u", "A", 0, 0), ("rs1_u", "A", 0, 3),
    ("expert", 1, 0), ("ag2_relay", "A", 1, 2), ("expert", 0, 2), ("rs1_t", "A", 0, 2), ("rs1_t", "B", 0),
    ("expert", 1, 1), ("rs1_t", "A", 0, 1), ("rs1_u", "B", 0), ("rs1_t", "A", 0, 3), ("expert", 1, 3),
    ("rs1_u", "A", 1, 2), ("rs1_u", "A", 1, 3), ("expert", 1, 2), ("rs1_u", "B", 1), ("rs1_m", "A", 0, 2),
    ("rs1_t", "A", 1, 2), ("rs1_t", "B", 1), ("rs1_t", "A", 1, 3), ("rs1_m", "B", 0), ("rs1_t", "A", 1, 1),
    ("weight_grads", 1), ("rs1_m", "A", 0, 3), ("rs1_m", "A", 0, 1), ("rs1_f", "A", 0, 2), ("rs2_t", "A", 0),
    ("rs1_u", "A", 1, 0), ("weight_grads", 0), ("rs1_m", "B", 1), ("rs1_f", "B", 0), ("rs2_t", "B", 0),
    ("rs1_m", "A", 1, 1), ("rs1_f", "A", 0, 3), ("rs1_m", "A", 1, 3), ("rs1_m", "A", 1, 2), ("rs1_f", "A", 0, 1),
    ("rs2_u", "A", 0), ("rs1_u", "A", 1, 1), ("rs2_u", "B", 0), ("rs2_m", "A", 0), ("rs1_t", "A", 0, 0),
    ("rs1_t", "A", 1, 0), ("rs2_m", "B", 0), ("rs1_f", "B", 1), ("rs2_t", "B", 1), ("rs2_u", "B", 1),
    ("rs1_f", "A", 1, 3), ("rs1_f", "A", 1, 2), ("rs2_t", "A", 1), ("rs1_f", "A", 1, 1), ("rs2_u", "A", 1),
    ("rs1_m", "A", 0, 0), ("rs1_m", "A", 1, 0), ("rs2_f", "B", 0), ("rs2_m", "B", 1), ("rs2_m", "A", 1),
    ("rs1_f", "A", 0, 0), ("rs2_f", "A", 0), ("rs1_f", "A", 1, 0), ("rs2_f", "B", 1), ("rs2_f", "A", 1),
)


def dot(a, b):
    return lax.dot_general(a, b, (((1,), (0,)), ((), ())), preferred_element_type=F32)


def dot_nt(a, b):
    return lax.dot_general(a, b, (((1,), (1,)), ((), ())), preferred_element_type=F32)


def dot_tn(a, b):
    return lax.dot_general(a, b, (((0,), (0,)), ((), ())), preferred_element_type=F32)


def iota(shape, dim):
    return lax.broadcasted_iota(jnp.int32, shape, dim)


def piece_row(slot_off, half, k, t, i):
    return slot_off * 16 + half * 8 + k * 4 + t * 2 + i


def spread_index(r, me):
    off, k, t, i = r >> 4, (r >> 2) & 1, (r >> 1) & 1, r & 1
    owner = (me + off) & 15
    return (t * 2 + i) * 32 + 2 * owner + k


def block_index(r):
    off, k, t, i = r >> 4, (r >> 2) & 1, (r >> 1) & 1, r & 1
    return (k * 2 + t) * 32 + off * 2 + i


def one_hot(index_of, half, rows_are_pieces):
    shape = (256, 128) if rows_are_pieces else (128, 256)
    piece = iota(shape, 0 if rows_are_pieces else 1)
    other = iota(shape, 1 if rows_are_pieces else 0)
    hit = (index_of(piece) == other) & (((piece >> 3) & 1) == half)
    return jnp.where(hit, 1.0, 0.0).astype(BF)


def kernel(
    patches_hbm, cot_hbm, ols_ref, keys_ref, win_hbm, wout_hbm,
    pg, kg_ref, wig, wog,
    patches, cot, win, wout,
    disp_s, comb_s, g, pt, act_s, pre_s, r1, r2,
    a2s, a2r, b2s, b2r, ks, k1, k2, k3,
    send_sem, recv_sem, in_sem,
):
    dp = lax.axis_index("dp")
    me = lax.axis_index("expert")
    zh, y = dp // 4, dp % 4

    def expert_peer(off):
        return (dp, lax.rem(me + off, 16))

    def dp_peer(off):
        return (lax.rem(dp + off, 16), me)

    def ring_peer(axis, step):
        if axis == "y":
            return (zh * 4 + lax.rem(y + step + 4, 4), me)
        return (lax.rem(zh + step + 4, 4) * 4 + y, me)

    barrier = pltpu.get_barrier_semaphore()
    for off in range(1, 16):
        pl.semaphore_signal(barrier, inc=1, device_id=expert_peer(off), device_id_type=MESH)
        pl.semaphore_signal(barrier, inc=1, device_id=dp_peer(off), device_id_type=MESH)

    loads = {}
    for n, (name, src, dst) in enumerate(
        (("x", patches_hbm, patches), ("c", cot_hbm, cot), ("wi", win_hbm, win), ("wo", wout_hbm, wout))
    ):
        loads[name] = pltpu.make_async_copy(src, dst, in_sem.at[n])
    loads["x"].start()
    loads["c"].start()

    recv_of, send_of, waited = {}, {}, set()

    def send(group, out, src, dst, device):
        n = recv_of.setdefault(group, len(recv_of))
        m = send_of.setdefault(out, len(send_of))
        assert n < N_RECV and m < N_SEND
        pltpu.make_async_remote_copy(
            src_ref=src, dst_ref=dst, send_sem=send_sem.at[m], recv_sem=recv_sem.at[n],
            device_id=device, device_id_type=MESH,
        ).start()

    def total_of(ref, n, m):
        return pltpu.make_async_remote_copy(
            src_ref=ref, dst_ref=ref, send_sem=send_sem.at[m], recv_sem=recv_sem.at[n],
            device_id=expert_peer(1), device_id_type=MESH,
        )

    def got(group, ref):
        if group not in waited:
            waited.add(group)
            total_of(ref, recv_of[group], 0).wait_recv()

    def sent(out, ref):
        total_of(ref, 0, send_of.pop(out)).wait_send()

    keys = keys_ref[...]
    loads["x"].wait()
    loads["c"].wait()
    loads["wi"].start()
    loads["wo"].start()
    rows_in, rows_grad = [], []
    for i in range(2):
        exponent = jnp.exp(dot_nt(keys, patches[i]))
        dispatch = exponent / jnp.sum(exponent, axis=1, keepdims=True)
        combine = exponent / (jnp.sum(exponent, axis=0, keepdims=True) + jnp.exp(ols_ref[i : i + 1, :]))
        disp_s[i] = dispatch
        comb_s[i] = combine
        rows_in.append(dot(dispatch.astype(BF), patches[i]).astype(BF))
        rows_grad.append(dot(combine.astype(BF), cot[i]).astype(BF))
    rows = jnp.concatenate(rows_in + rows_grad, axis=0)

    def to_pieces(rows, index_of, dst):
        half = D // 2
        pieces = dot(one_hot(index_of, 0, True), rows[:, :half]) + dot(
            one_hot(index_of, 1, True), rows[:, half:]
        )
        dst[...] = pieces.astype(BF).reshape(16, 16, half)

    def from_pieces(src, index_of, half):
        pieces = src[...].reshape(256, D // 2)
        return dot(one_hot(index_of, half, False), pieces).astype(BF)

    spread = functools.partial(spread_index, me=me)
    to_pieces(rows, spread, a2s)
    a2r[0] = a2s[0]
    pl.semaphore_wait(barrier, 30)
    for off in range(1, 16):
        send("a", "a", a2s.at[off], a2r.at[off], expert_peer(off))
    got("a", a2r.at[pl.ds(1, 15)])
    for half in range(2):
        cols = slice(half * 640, half * 640 + 640)
        g[:, 0, 0, :, cols] = from_pieces(a2r, block_index, half).reshape(4, 32, 640)

    AXES = {"A": ("z", "y"), "B": ("y", "z")}

    def cols_of(part):
        return pl.ds(*COLS[part])

    def at(ref, part, k, a1, a2, r0=0, nr=32):
        dy, dz = (a2, a1) if part == "A" else (a1, a2)
        return ref.at[pl.ds(2 * k, 2), dy, dz, pl.ds(r0, nr), cols_of(part)]

    def two(part, k):
        return g.at[pl.ds(2 * k, 2), 0, pl.ds(0, 2), :, cols_of(part)]

    def ag1(part, k):
        for step, a in ((1, 3), (-1, 1)):
            send(("p1", part, k), "ag1", at(g, part, k, 0, 0), at(g, part, k, a, 0), ring_peer(AXES[part][0], step))

    def ag1_relay(part, k):
        got(("p1", part, k), two(part, k))
        for step, a, r in ((1, 3, 0), (-1, 1, 16)):
            send(("r1", part, k), "ag1", at(g, part, k, a, 0, r, 16), at(g, part, k, 2, 0, r, 16), ring_peer(AXES[part][0], step))

    def first_in(part, k, a1):
        if a1 in (1, 3):
            got(("p1", part, k), two(part, k))
        if a1 == 2:
            got(("r1", part, k), at(g, part, k, 2, 0))

    def ag2(part, k, a1):
        first_in(part, k, a1)
        for step, a in ((1, 3), (-1, 1)):
            send(("p2", part, k, a1), "ag2", at(g, part, k, a1, 0), at(g, part, k, a1, a), ring_peer(AXES[part][1], step))

    def ag2_relay(part, k, a1):
        got(("p2", part, k, a1), two(part, k))
        for step, a, r in ((1, 3, 0), (-1, 1, 16)):
            send(("r2", part, k, a1), "ag2", at(g, part, k, a1, a, r, 16), at(g, part, k, a1, 2, r, 16), ring_peer(AXES[part][1], step))

    def slot_in(part, k, a1, a2):
        if a2 == 0:
            first_in(part, k, a1)
        elif a2 == 2:
            got(("r2", part, k, a1), at(g, part, k, a1, 2))
        else:
            got(("p2", part, k, a1), two(part, k))

    def expert(k, dy):
        for n in range(4):
            slot_in("A", k, n, dy)
            slot_in("B", k, dy, n)
        if "w" not in waited:
            waited.add("w")
            loads["wi"].wait()
            loads["wo"].wait()
        x0 = g[2 * k, dy].reshape(128, D)
        x1 = g[2 * k + 1, dy].reshape(128, D)
        hidden = dot_nt(x0, win[k])
        upstream = dot_nt(x1, wout[k])
        square = hidden * hidden
        tanh = jnp.tanh(GELU_C * (hidden + GELU_A * square * hidden))
        act = (0.5 * hidden * (1.0 + tanh)).astype(BF)
        slope = 0.5 * (1.0 + tanh) + (0.5 * hidden) * (1.0 - tanh * tanh) * (
            GELU_C + (3.0 * GELU_C * GELU_A) * square
        )
        pre = (slope * upstream).astype(BF)
        act_s[k, dy * 128 : dy * 128 + 128, :] = act
        pre_s[k, dy * 128 : dy * 128 + 128, :] = pre
        pt[2 * k, dy] = dot(act, wout[k]).astype(BF).reshape(4, 32, D)
        pt[2 * k + 1, dy] = dot(pre, win[k]).astype(BF).reshape(4, 32, D)

    def weight_grads(k):
        wog[k] = dot_tn(act_s[k], g[2 * k + 1].reshape(512, D)).astype(BF)
        wig[k] = dot_tn(pre_s[k], g[2 * k].reshape(512, D)).astype(BF)

    TP, TM, UP, MP, UM, MM = range(6)

    def part_of(ph, part, k, a1, a2, r0):
        if ph == 1 and part == "B":
            return pt.at[pl.ds(2 * k, 2), :, a2, pl.ds(r0, 16), cols_of(part)]
        if ph == 1:
            return at(pt, part, k, a1, a2, r0, 16)
        return at(pt, part, k, a2, 0, r0, 16)

    def land(ph, part, k, a1, m):
        if ph == 1:
            return r1.at[k, m, :, slice(None) if part == "B" else a1, :, cols_of(part)]
        return r2.at[k, m, :, :, cols_of(part)]

    def rs_send(ph, part, k, a1, m, a2, r0):
        step = 1 if m in (TP, UP, MP) else -1
        kind = "t" if m < 2 else "u"
        send((kind, ph, part, k, a1), ("rs", ph), part_of(ph, part, k, a1, a2, r0), land(ph, part, k, a1, m), ring_peer(AXES[part][2 - ph], step))

    def rs_got(ph, part, k, a1, kind):
        m = pl.ds(0, 2) if kind == "t" else pl.ds(2, 4)
        got((kind, ph, part, k, a1), land(ph, part, k, a1, m))

    def rs_t(ph, part, k, a1=None):
        rs_send(ph, part, k, a1, TP, 2, 16)
        rs_send(ph, part, k, a1, TM, 2, 0)

    def rs_u(ph, part, k, a1=None):
        rs_send(ph, part, k, a1, UP, 1, 0)
        rs_send(ph, part, k, a1, UM, 3, 16)

    def add_into(dst, *srcs):
        total = dst[...].astype(F32)
        for src in srcs:
            total = total + src[...].astype(F32)
        dst[...] = total.astype(BF)

    def rs_m(ph, part, k, a1=None):
        rs_got(ph, part, k, a1, "t")
        for t, m, a2, r0 in ((TP, MP, 1, 16), (TM, MM, 3, 0)):
            add_into(part_of(ph, part, k, a1, a2, r0), land(ph, part, k, a1, t))
            rs_send(ph, part, k, a1, m, a2, r0)

    def rs_f(ph, part, k, a1=None):
        rs_got(ph, part, k, a1, "u")
        for u, m, r0 in ((UP, MM, 0), (UM, MP, 16)):
            add_into(part_of(ph, part, k, a1, 0, r0), land(ph, part, k, a1, u), land(ph, part, k, a1, m))

    steps = {"ag1": ag1, "ag1_relay": ag1_relay, "ag2": ag2, "ag2_relay": ag2_relay, "expert": expert, "weight_grads": weight_grads}
    for ph in (1, 2):
        for name, step in (("t", rs_t), ("u", rs_u), ("m", rs_m), ("f", rs_f)):
            steps["rs%d_%s" % (ph, name)] = functools.partial(step, ph)
    for name, *where in ORDER:
        steps[name](*where)

    to_pieces(pt[:, 0, 0].reshape(128, D), block_index, b2s)
    b2r[0] = b2s[0]
    for off in range(1, 16):
        send("b", "b", b2s.at[off], b2r.at[off], expert_peer(16 - off))
    got("b", b2r.at[pl.ds(1, 15)])
    back = jnp.concatenate([from_pieces(b2r, spread, half) for half in range(2)], axis=1)

    halves = []
    key_part = jnp.zeros((32, D), F32)
    for i in range(2):
        slot_out = back[i * 32 : i * 32 + 32]
        slot_in_grad = back[64 + i * 32 : 96 + i * 32]
        comb_grad = dot_nt(slot_out, cot[i])
        disp_grad = dot_nt(slot_in_grad, patches[i])
        dispatch = disp_s[i]
        combine = comb_s[i]
        logit_grad = combine * (comb_grad - jnp.sum(combine * comb_grad, axis=0, keepdims=True))
        logit_grad = logit_grad + dispatch * (
            disp_grad - jnp.sum(dispatch * disp_grad, axis=1, keepdims=True)
        )
        logit_half = logit_grad.astype(BF)
        key_part = key_part + dot(logit_half, patches[i])
        halves.append((dispatch.astype(BF), logit_half, slot_in_grad))

    def piece(o):
        return slice(o // 5 * 16, o // 5 * 16 + 16), slice(o % 5 * 256, o % 5 * 256 + 256)

    owner = me < OWNERS
    for o in range(OWNERS):
        ks[o] = key_part[piece(o)].astype(BF)

        @pl.when(me != o)
        def _():
            send("k1", "k1", ks.at[o], k1.at[me], (dp, o))

    def image_out(i):
        dispatch_half, logit_half, slot_in_grad = halves[i]
        lhs = jnp.concatenate([dispatch_half, logit_half], axis=0)
        rhs = jnp.concatenate([slot_in_grad, keys], axis=0)
        pg[i] = dot_tn(lhs, rhs).astype(BF)

    image_out(0)

    @pl.when(owner)
    def _():
        k1[me] = ks[me]
        got("k1", k1.at[pl.ds(1, 15)])
        total = k1[0].astype(F32)
        for n in range(1, 16):
            total = total + k1[n].astype(F32)
        k2[dp] = total.astype(BF)
        for off in range(1, 16):
            send("k2", "k2", k2.at[dp], k2.at[dp], dp_peer(off))

    image_out(1)

    @pl.when(owner)
    def _():
        got("k2", k2.at[pl.ds(1, 15)])
        total = k2[0].astype(F32)
        for n in range(1, 16):
            total = total + k2[n].astype(F32)
        k3[me] = total.astype(BF)
        for off in range(1, 16):
            send("k3", "k3", k3.at[me], k3.at[me], expert_peer(off))

    n_k1, n_k3 = send_of["k1"], recv_of["k3"]
    waited.add("k3")

    @pl.when(owner)
    def _():
        total_of(k3.at[pl.ds(0, OWNERS - 1)], n_k3, 0).wait_recv()

    @pl.when(jnp.logical_not(owner))
    def _():
        total_of(k3, n_k3, 0).wait_recv()

    for o in range(OWNERS):
        kg_ref[piece(o)] = k3[o].astype(F32)

    @pl.when(owner)
    def _():
        total_of(ks.at[pl.ds(0, OWNERS - 1)], 0, n_k1).wait_send()
        sent("k2", k2.at[pl.ds(1, 15)])
        sent("k3", k1.at[pl.ds(1, 15)])

    @pl.when(jnp.logical_not(owner))
    def _():
        total_of(ks, 0, send_of.pop("k1")).wait_send()

    for out, ref in (("a", a2s), ("b", b2s)):
        sent(out, ref.at[pl.ds(1, 15)])
    sent("ag1", g.at[:, 0, pl.ds(1, 3)])
    sent("ag2", g.at[:, pl.ds(1, 3)])
    sent(("rs", 1), r1)
    sent(("rs", 2), r2)
    assert not send_of and len(waited) == len(recv_of) + 1


def write_out(*refs):
    copies = [pltpu.make_async_copy(refs[n], refs[n + 4], refs[8].at[n]) for n in range(4)]
    for copy in copies:
        copy.start()
    for copy in copies:
        copy.wait()


def on_device(patches, cotangent, other_logsum, slot_keys, w_in, w_out):
    any_spec = pl.BlockSpec(memory_space=pl.ANY)
    vmem = pl.BlockSpec(memory_space=pltpu.VMEM)
    results = pl.pallas_call(
        kernel,
        out_shape=(
            pltpu.VMEM((2, 256, D), BF),
            pltpu.VMEM((32, D), F32),
            pltpu.VMEM((2, FB, D), BF),
            pltpu.VMEM((2, FB, D), BF),
        ),
        in_specs=[any_spec, any_spec, vmem, vmem, any_spec, any_spec],
        out_specs=(vmem, vmem, vmem, vmem),
        scratch_shapes=[
            pltpu.VMEM((2, 256, D), BF),
            pltpu.VMEM((2, 256, D), BF),
            pltpu.VMEM((2, FB, D), BF),
            pltpu.VMEM((2, FB, D), BF),
            pltpu.VMEM((2, 32, 256), F32),
            pltpu.VMEM((2, 32, 256), F32),
            pltpu.VMEM((4, 4, 4, 32, D), BF),
            pltpu.VMEM((4, 4, 4, 32, D), BF),
            pltpu.VMEM((2, 512, FB), BF),
            pltpu.VMEM((2, 512, FB), BF),
            pltpu.VMEM((2, 6, 2, 4, 16, D), BF),
            pltpu.VMEM((2, 6, 2, 16, D), BF),
            pltpu.VMEM((16, 16, D // 2), BF),
            pltpu.VMEM((16, 16, D // 2), BF),
            pltpu.VMEM((16, 16, D // 2), BF),
            pltpu.VMEM((16, 16, D // 2), BF),
            pltpu.VMEM((OWNERS, 16, 256), BF),
            pltpu.VMEM((16, 16, 256), BF),
            pltpu.VMEM((16, 16, 256), BF),
            pltpu.VMEM((OWNERS, 16, 256), BF),
            pltpu.SemaphoreType.DMA((N_SEND,)),
            pltpu.SemaphoreType.DMA((N_RECV,)),
            pltpu.SemaphoreType.DMA((4,)),
        ],
        compiler_params=pltpu.CompilerParams(
            collective_id=0, has_side_effects=True, vmem_limit_bytes=58 * 2**20
        ),
        name="soft_moe_backward",
    )(patches, cotangent, other_logsum, slot_keys, jnp.swapaxes(w_in, 1, 2), w_out)
    patch_grad, key_grad, w_in_grad, w_out_grad = pl.pallas_call(
        write_out,
        out_shape=[jax.ShapeDtypeStruct(r.shape, r.dtype) for r in results],
        in_specs=[vmem] * 4,
        out_specs=[any_spec] * 4,
        scratch_shapes=[pltpu.SemaphoreType.DMA((4,))],
        name="write_out",
    )(*results)
    return (patch_grad, key_grad, jnp.swapaxes(w_in_grad, 1, 2), w_out_grad)


def solution(mesh):
    placed = (
        P(("dp", "expert"), None, None),
        P(("dp", "expert"), None, None),
        P(("dp", "expert"), None),
        P(),
        P("expert", None, "dp"),
        P("expert", "dp", None),
    )
    return jax.shard_map(
        on_device,
        mesh=mesh,
        in_specs=placed,
        out_specs=(
            P(("dp", "expert"), None, None),
            P(),
            P("expert", None, "dp"),
            P("expert", "dp", None),
        ),
        check_vma=False,
    )
```

```python
import functools

import jax
import jax.numpy as jnp
from jax import lax
from jax.experimental import pallas as pl
from jax.experimental.pallas import tpu as pltpu
from jax.sharding import PartitionSpec as P

MESH = pl.DeviceIdType.MESH
BF = jnp.bfloat16
F32 = jnp.float32

D = 1280
FB = 320
SPLIT = 1024
COLS = {"A": (0, SPLIT), "B": (SPLIT, D - SPLIT)}
N_RECV = 80
N_SEND = 12
WINDOWS = (0, 384, 768, 896)
OWNERS = 10
GELU_C = 0.7978845608028654
GELU_A = 0.044715

ORDER = (
    ("a_got", 0), ("ag1", "A", 0), ("ag1", "B", 0), ("ag2", "A", 0, 0), ("a_got", 1), ("ag1_relay", "B", 0),
    ("ag1", "B", 1), ("ag2", "B", 0, 0), ("ag2", "A", 1, 0), ("ag2", "B", 0, 3), ("ag2_relay", "A", 0, 0),
    ("ag1_relay", "B", 1), ("ag2", "B", 0, 2), ("ag1_relay", "A", 0), ("ag2", "A", 0, 3), ("ag2", "A", 0, 1),
    ("ag1", "A", 1), ("ag2_relay", "A", 1, 0), ("ag2_relay", "B", 0, 0), ("ag2", "A", 0, 2), ("ag2", "B", 0, 1),
    ("ag2_relay", "A", 0, 1), ("ag2_relay", "A", 0, 3), ("ag2", "B", 1, 1), ("ag2_relay", "B", 0, 2),
    ("ag2_relay", "B", 0, 3), ("ag2", "B", 1, 0), ("ag2_relay", "A", 0, 2), ("ag1_relay", "A", 1),
    ("ag2", "A", 1, 1), ("expert", 0, 0), ("ag2_relay", "B", 0, 1), ("ag2", "B", 1, 2), ("ag2", "B", 1, 3),
    ("ag2", "A", 1, 3), ("expert", 0, 2), ("ag2_relay", "B", 1, 0), ("rs1_t", "A", 0, 2), ("ag2_relay", "B", 1, 1),
    ("ag2_relay", "A", 1, 1), ("expert", 0, 3), ("ag2", "A", 1, 2), ("expert", 0, 1), ("ag2_relay", "B", 1, 2),
    ("rs1_t", "B", 0), ("rs1_u", "A", 0, 2), ("rs1_m", "A", 0, 2), ("ag2_relay", "A", 1, 3), ("expert", 1, 0),
    ("ag2_relay", "A", 1, 2), ("rs1_t", "A", 0, 1), ("rs1_u", "B", 0), ("ag2_relay", "B", 1, 3),
    ("rs1_t", "A", 0, 3), ("expert", 1, 1), ("rs1_f", "A", 0, 2), ("rs1_m", "B", 0), ("rs2_t", "A", 0),
    ("rs1_u", "A", 0, 3), ("rs1_u", "A", 0, 1), ("expert", 1, 2), ("rs1_t", "A", 1, 2), ("rs1_t", "A", 1, 1),
    ("expert", 1, 3), ("rs1_t", "B", 1), ("rs1_u", "A", 1, 2), ("rs1_t", "A", 1, 3), ("rs1_m", "A", 1, 2),
    ("rs1_m", "A", 0, 3), ("rs1_u", "B", 1), ("rs1_m", "A", 0, 1), ("rs1_f", "B", 0), ("rs1_m", "A", 1, 1),
    ("rs1_u", "A", 1, 3), ("rs1_m", "B", 1), ("rs1_m", "A", 1, 3), ("rs2_u", "B", 0), ("rs2_t", "B", 0),
    ("rs1_u", "A", 1, 1), ("rs1_t", "A", 0, 0), ("rs1_f", "A", 1, 2), ("rs1_t", "A", 1, 0), ("rs2_t", "A", 1),
    ("rs1_f", "A", 0, 3), ("rs1_u", "A", 0, 0), ("rs1_f", "A", 0, 1), ("rs2_m", "A", 0), ("rs2_u", "A", 0),
    ("weight_grads", 0), ("rs1_f", "B", 1), ("rs1_f", "A", 1, 3), ("rs2_t", "B", 1), ("rs1_f", "A", 1, 1),
    ("rs2_u", "A", 1), ("rs2_m", "A", 1), ("rs2_m", "B", 0), ("rs1_m", "A", 0, 0), ("rs1_m", "A", 1, 0),
    ("rs1_u", "A", 1, 0), ("rs2_m", "B", 1), ("rs2_f", "B", 0), ("rs2_u", "B", 1), ("rs1_f", "A", 0, 0),
    ("rs2_f", "A", 0), ("b_send", 0), ("rs1_f", "A", 1, 0), ("rs2_f", "B", 1), ("rs2_f", "A", 1), ("b_send", 1),
    ("weight_grads", 1),
)


def dot(a, b):
    return lax.dot_general(a, b, (((1,), (0,)), ((), ())), preferred_element_type=F32)


def dot_nt(a, b):
    return lax.dot_general(a, b, (((1,), (1,)), ((), ())), preferred_element_type=F32)


def dot_tn(a, b):
    return lax.dot_general(a, b, (((0,), (0,)), ((), ())), preferred_element_type=F32)


def iota(shape, dim):
    return lax.broadcasted_iota(jnp.int32, shape, dim)


def piece_parts(r):
    return r >> 4, (r >> 2) & 3, (r >> 1) & 1, r & 1


def one_hot(index_of, window, others, pieces_first):
    shape = (256, others) if pieces_first else (others, 256)
    piece = iota(shape, 0 if pieces_first else 1)
    other = iota(shape, 1 if pieces_first else 0)
    hit = (index_of(piece) == other) & (piece_parts(piece)[1] == window)
    return jnp.where(hit, 1.0, 0.0).astype(BF)


def kernel(
    patches_hbm, cot_hbm, ols_ref, keys_ref, win_hbm, wout_hbm,
    pg, kg_ref, wig, wog,
    patches, cot, win, wout,
    disp_s, comb_s, g, pt, act_s, pre_s, r1, r2,
    a2s, a2r, b2s, b2r, ks, k1, k2, k3,
    send_sem, recv_sem, in_sem,
):
    dp = lax.axis_index("dp")
    me = lax.axis_index("expert")
    zh, y = dp // 4, dp % 4

    def expert_peer(off):
        return (dp, lax.rem(me + off, 16))

    def dp_peer(off):
        return (lax.rem(dp + off, 16), me)

    def ring_peer(axis, step):
        if axis == "y":
            return (zh * 4 + lax.rem(y + step + 4, 4), me)
        return (lax.rem(zh + step + 4, 4) * 4 + y, me)

    barrier = pltpu.get_barrier_semaphore()
    for off in range(1, 16):
        pl.semaphore_signal(barrier, inc=1, device_id=expert_peer(off), device_id_type=MESH)
        pl.semaphore_signal(barrier, inc=1, device_id=dp_peer(off), device_id_type=MESH)

    loads = {}
    for n, (name, src, dst) in enumerate(
        (("x", patches_hbm, patches), ("c", cot_hbm, cot), ("wi", win_hbm, win), ("wo", wout_hbm, wout))
    ):
        loads[name] = pltpu.make_async_copy(src, dst, in_sem.at[n])
    loads["x"].start()
    loads["c"].start()

    recv_of, send_of, waited = {}, {}, set()

    def send(group, out, src, dst, device):
        n = recv_of.setdefault(group, len(recv_of))
        m = send_of.setdefault(out, len(send_of))
        assert n < N_RECV and m < N_SEND
        pltpu.make_async_remote_copy(
            src_ref=src, dst_ref=dst, send_sem=send_sem.at[m], recv_sem=recv_sem.at[n],
            device_id=device, device_id_type=MESH,
        ).start()

    def total_of(ref, n, m):
        return pltpu.make_async_remote_copy(
            src_ref=ref, dst_ref=ref, send_sem=send_sem.at[m], recv_sem=recv_sem.at[n],
            device_id=expert_peer(1), device_id_type=MESH,
        )

    def got(group, ref):
        if group not in waited:
            waited.add(group)
            total_of(ref, recv_of[group], 0).wait_recv()

    def sent(out, ref):
        total_of(ref, 0, send_of.pop(out)).wait_send()

    keys = keys_ref[...]
    loads["x"].wait()
    loads["c"].wait()
    loads["wi"].start()
    loads["wo"].start()
    rows_in, rows_grad = [], []
    for i in range(2):
        exponent = jnp.exp(dot_nt(keys, patches[i]))
        dispatch = exponent / jnp.sum(exponent, axis=1, keepdims=True)
        combine = exponent / (jnp.sum(exponent, axis=0, keepdims=True) + jnp.exp(ols_ref[i : i + 1, :]))
        disp_s[i] = dispatch
        comb_s[i] = combine
        rows_in.append(dot(dispatch.astype(BF), patches[i]).astype(BF))
        rows_grad.append(dot(combine.astype(BF), cot[i]).astype(BF))
    rows = jnp.concatenate(rows_in + rows_grad, axis=0)

    def spread(k):
        def index(r):
            off, _, t, i = piece_parts(r)
            return (t * 2 + i) * 32 + 2 * ((me + off) & 15) + k

        return index

    def in_block(r):
        off, _, t, i = piece_parts(r)
        return t * 32 + off * 2 + i

    def to_pieces(rows, index_of, dst):
        total = jnp.zeros((256, 384), F32)
        for w, c0 in enumerate(WINDOWS):
            total = total + dot(one_hot(index_of, w, rows.shape[0], True), rows[:, c0 : c0 + 384])
        dst[...] = total.astype(BF).reshape(16, 16, 384)

    def from_pieces(src, index_of, window, others):
        return dot(one_hot(index_of, window, others, False), src[...].reshape(256, 384))

    pl.semaphore_wait(barrier, 30)
    for k in range(2):
        to_pieces(rows, spread(k), a2s.at[k])
        a2r[k, 0] = a2s[k, 0]
        for off in range(1, 16):
            send(("a", k), ("a", k), a2s.at[k, off], a2r.at[k, off], expert_peer(off))

    def a_got(k):
        got(("a", k), a2r.at[k, pl.ds(1, 15)])
        for w, c0 in enumerate(WINDOWS):
            block = from_pieces(a2r.at[k], in_block, w, 64).astype(BF)
            if w == 3:
                block, c0 = block[:, 256:], c0 + 256
            g[2 * k : 2 * k + 2, 0, 0, :, c0 : c0 + block.shape[1]] = block.reshape(2, 32, block.shape[1])

    def b_send(k):
        to_pieces(pt[2 * k : 2 * k + 2, 0, 0].reshape(64, D), in_block, b2s.at[k])
        b2r[k, 0] = b2s[k, 0]
        for off in range(1, 16):
            send(("b", k), ("b", k), b2s.at[k, off], b2r.at[k, off], expert_peer(16 - off))

    AXES = {"A": ("z", "y"), "B": ("y", "z")}

    def cols_of(part):
        return pl.ds(*COLS[part])

    def at(ref, part, k, a1, a2, r0=0, nr=32):
        dy, dz = (a2, a1) if part == "A" else (a1, a2)
        return ref.at[pl.ds(2 * k, 2), dy, dz, pl.ds(r0, nr), cols_of(part)]

    def two(part, k):
        return g.at[pl.ds(2 * k, 2), 0, pl.ds(0, 2), :, cols_of(part)]

    def ag1(part, k):
        for step, a in ((1, 3), (-1, 1)):
            send(("p1", part, k), "ag1", at(g, part, k, 0, 0), at(g, part, k, a, 0), ring_peer(AXES[part][0], step))

    def ag1_relay(part, k):
        got(("p1", part, k), two(part, k))
        for step, a, r in ((1, 3, 0), (-1, 1, 16)):
            send(("r1", part, k), "ag1", at(g, part, k, a, 0, r, 16), at(g, part, k, 2, 0, r, 16), ring_peer(AXES[part][0], step))

    def first_in(part, k, a1):
        if a1 in (1, 3):
            got(("p1", part, k), two(part, k))
        if a1 == 2:
            got(("r1", part, k), at(g, part, k, 2, 0))

    def ag2(part, k, a1):
        first_in(part, k, a1)
        for step, a in ((1, 3), (-1, 1)):
            send(("p2", part, k, a1), "ag2", at(g, part, k, a1, 0), at(g, part, k, a1, a), ring_peer(AXES[part][1], step))

    def ag2_relay(part, k, a1):
        got(("p2", part, k, a1), two(part, k))
        for step, a, r in ((1, 3, 0), (-1, 1, 16)):
            send(("r2", part, k, a1), "ag2", at(g, part, k, a1, a, r, 16), at(g, part, k, a1, 2, r, 16), ring_peer(AXES[part][1], step))

    def slot_in(part, k, a1, a2):
        if a2 == 0:
            first_in(part, k, a1)
        elif a2 == 2:
            got(("r2", part, k, a1), at(g, part, k, a1, 2))
        else:
            got(("p2", part, k, a1), two(part, k))

    def expert(k, dy):
        for n in range(4):
            slot_in("A", k, n, dy)
            slot_in("B", k, dy, n)
        if "w" not in waited:
            waited.add("w")
            loads["wi"].wait()
            loads["wo"].wait()
        x0 = g[2 * k, dy].reshape(128, D)
        x1 = g[2 * k + 1, dy].reshape(128, D)
        hidden = dot_nt(x0, win[k])
        upstream = dot_nt(x1, wout[k])
        square = hidden * hidden
        tanh = jnp.tanh(GELU_C * (hidden + GELU_A * square * hidden))
        act = (0.5 * hidden * (1.0 + tanh)).astype(BF)
        slope = 0.5 * (1.0 + tanh) + (0.5 * hidden) * (1.0 - tanh * tanh) * (
            GELU_C + (3.0 * GELU_C * GELU_A) * square
        )
        pre = (slope * upstream).astype(BF)
        act_s[k, dy * 128 : dy * 128 + 128, :] = act
        pre_s[k, dy * 128 : dy * 128 + 128, :] = pre
        pt[2 * k, dy] = dot(act, wout[k]).astype(BF).reshape(4, 32, D)
        pt[2 * k + 1, dy] = dot(pre, win[k]).astype(BF).reshape(4, 32, D)

    def weight_grads(k):
        wog[k] = dot_tn(act_s[k], g[2 * k + 1].reshape(512, D)).astype(BF)
        wig[k] = dot_tn(pre_s[k], g[2 * k].reshape(512, D)).astype(BF)

    TP, TM, UP, MP, UM, MM = range(6)

    def part_of(ph, part, k, a1, a2, r0):
        if ph == 1 and part == "B":
            return pt.at[pl.ds(2 * k, 2), :, a2, pl.ds(r0, 16), cols_of(part)]
        if ph == 1:
            return at(pt, part, k, a1, a2, r0, 16)
        return at(pt, part, k, a2, 0, r0, 16)

    def land(ph, part, k, a1, m):
        if ph == 1:
            return r1.at[k, m, :, slice(None) if part == "B" else a1, :, cols_of(part)]
        return r2.at[k, m, :, :, cols_of(part)]

    def rs_send(ph, part, k, a1, m, a2, r0):
        step = 1 if m in (TP, UP, MP) else -1
        kind = "t" if m < 2 else "u"
        send((kind, ph, part, k, a1), ("rs", ph), part_of(ph, part, k, a1, a2, r0), land(ph, part, k, a1, m), ring_peer(AXES[part][2 - ph], step))

    def rs_got(ph, part, k, a1, kind):
        m = pl.ds(0, 2) if kind == "t" else pl.ds(2, 4)
        got((kind, ph, part, k, a1), land(ph, part, k, a1, m))

    def rs_t(ph, part, k, a1=None):
        rs_send(ph, part, k, a1, TP, 2, 16)
        rs_send(ph, part, k, a1, TM, 2, 0)

    def rs_u(ph, part, k, a1=None):
        rs_send(ph, part, k, a1, UP, 1, 0)
        rs_send(ph, part, k, a1, UM, 3, 16)

    def add_into(dst, *srcs):
        total = dst[...].astype(F32)
        for src in srcs:
            total = total + src[...].astype(F32)
        dst[...] = total.astype(BF)

    def rs_m(ph, part, k, a1=None):
        rs_got(ph, part, k, a1, "t")
        for t, m, a2, r0 in ((TP, MP, 1, 16), (TM, MM, 3, 0)):
            add_into(part_of(ph, part, k, a1, a2, r0), land(ph, part, k, a1, t))
            rs_send(ph, part, k, a1, m, a2, r0)

    def rs_f(ph, part, k, a1=None):
        rs_got(ph, part, k, a1, "u")
        for u, m, r0 in ((UP, MM, 0), (UM, MP, 16)):
            add_into(part_of(ph, part, k, a1, 0, r0), land(ph, part, k, a1, u), land(ph, part, k, a1, m))

    steps = {"ag1": ag1, "ag1_relay": ag1_relay, "ag2": ag2, "ag2_relay": ag2_relay, "expert": expert, "weight_grads": weight_grads, "a_got": a_got, "b_send": b_send}
    for ph in (1, 2):
        for name, step in (("t", rs_t), ("u", rs_u), ("m", rs_m), ("f", rs_f)):
            steps["rs%d_%s" % (ph, name)] = functools.partial(step, ph)
    for name, *where in ORDER:
        steps[name](*where)

    for k in range(2):
        got(("b", k), b2r.at[k, pl.ds(1, 15)])
    back = []
    for w in range(4):
        cols = sum(from_pieces(b2r.at[k], spread(k), w, 128) for k in range(2)).astype(BF)
        back.append(cols[:, 256:] if w == 3 else cols)
    back = jnp.concatenate(back, axis=1)

    halves = []
    key_part = jnp.zeros((32, D), F32)
    for i in range(2):
        slot_out = back[i * 32 : i * 32 + 32]
        slot_in_grad = back[64 + i * 32 : 96 + i * 32]
        comb_grad = dot_nt(slot_out, cot[i])
        disp_grad = dot_nt(slot_in_grad, patches[i])
        dispatch = disp_s[i]
        combine = comb_s[i]
        logit_grad = combine * (comb_grad - jnp.sum(combine * comb_grad, axis=0, keepdims=True))
        logit_grad = logit_grad + dispatch * (
            disp_grad - jnp.sum(dispatch * disp_grad, axis=1, keepdims=True)
        )
        logit_half = logit_grad.astype(BF)
        key_part = key_part + dot(logit_half, patches[i])
        halves.append((dispatch.astype(BF), logit_half, slot_in_grad))

    def piece(o):
        return slice(o // 5 * 16, o // 5 * 16 + 16), slice(o % 5 * 256, o % 5 * 256 + 256)

    owner = me < OWNERS
    for o in range(OWNERS):
        ks[o] = key_part[piece(o)].astype(BF)

        @pl.when(me != o)
        def _():
            send("k1", "k1", ks.at[o], k1.at[me], (dp, o))

    def image_out(i):
        dispatch_half, logit_half, slot_in_grad = halves[i]
        lhs = jnp.concatenate([dispatch_half, logit_half], axis=0)
        rhs = jnp.concatenate([slot_in_grad, keys], axis=0)
        pg[i] = dot_tn(lhs, rhs).astype(BF)

    image_out(0)

    @pl.when(owner)
    def _():
        k1[me] = ks[me]
        got("k1", k1.at[pl.ds(1, 15)])
        total = k1[0].astype(F32)
        for n in range(1, 16):
            total = total + k1[n].astype(F32)
        k2[dp] = total.astype(BF)
        for off in range(1, 16):
            send("k2", "k2", k2.at[dp], k2.at[dp], dp_peer(off))

    image_out(1)

    @pl.when(owner)
    def _():
        got("k2", k2.at[pl.ds(1, 15)])
        total = k2[0].astype(F32)
        for n in range(1, 16):
            total = total + k2[n].astype(F32)
        k3[me] = total.astype(BF)
        for off in range(1, 16):
            send("k3", "k3", k3.at[me], k3.at[me], expert_peer(off))

    n_k1, n_k3 = send_of["k1"], recv_of["k3"]
    waited.add("k3")

    @pl.when(owner)
    def _():
        total_of(k3.at[pl.ds(0, OWNERS - 1)], n_k3, 0).wait_recv()

    @pl.when(jnp.logical_not(owner))
    def _():
        total_of(k3, n_k3, 0).wait_recv()

    for o in range(OWNERS):
        kg_ref[piece(o)] = k3[o].astype(F32)

    @pl.when(owner)
    def _():
        total_of(ks.at[pl.ds(0, OWNERS - 1)], 0, n_k1).wait_send()
        sent("k2", k2.at[pl.ds(1, 15)])
        sent("k3", k1.at[pl.ds(1, 15)])

    @pl.when(jnp.logical_not(owner))
    def _():
        total_of(ks, 0, send_of.pop("k1")).wait_send()

    for k in range(2):
        sent(("a", k), a2s.at[k, pl.ds(1, 15)])
        sent(("b", k), b2s.at[k, pl.ds(1, 15)])
    sent("ag1", g.at[:, 0, pl.ds(1, 3)])
    sent("ag2", g.at[:, pl.ds(1, 3)])
    sent(("rs", 1), r1)
    sent(("rs", 2), r2)
    assert not send_of and len(waited) == len(recv_of) + 1


def write_out(*refs):
    copies = [pltpu.make_async_copy(refs[n], refs[n + 4], refs[8].at[n]) for n in range(4)]
    for copy in copies:
        copy.start()
    for copy in copies:
        copy.wait()


def on_device(patches, cotangent, other_logsum, slot_keys, w_in, w_out):
    any_spec = pl.BlockSpec(memory_space=pl.ANY)
    vmem = pl.BlockSpec(memory_space=pltpu.VMEM)
    results = pl.pallas_call(
        kernel,
        out_shape=(
            pltpu.VMEM((2, 256, D), BF),
            pltpu.VMEM((32, D), F32),
            pltpu.VMEM((2, FB, D), BF),
            pltpu.VMEM((2, FB, D), BF),
        ),
        in_specs=[any_spec, any_spec, vmem, vmem, any_spec, any_spec],
        out_specs=(vmem, vmem, vmem, vmem),
        scratch_shapes=[
            pltpu.VMEM((2, 256, D), BF),
            pltpu.VMEM((2, 256, D), BF),
            pltpu.VMEM((2, FB, D), BF),
            pltpu.VMEM((2, FB, D), BF),
            pltpu.VMEM((2, 32, 256), F32),
            pltpu.VMEM((2, 32, 256), F32),
            pltpu.VMEM((4, 4, 4, 32, D), BF),
            pltpu.VMEM((4, 4, 4, 32, D), BF),
            pltpu.VMEM((2, 512, FB), BF),
            pltpu.VMEM((2, 512, FB), BF),
            pltpu.VMEM((2, 6, 2, 4, 16, D), BF),
            pltpu.VMEM((2, 6, 2, 16, D), BF),
            pltpu.VMEM((2, 16, 16, 384), BF),
            pltpu.VMEM((2, 16, 16, 384), BF),
            pltpu.VMEM((2, 16, 16, 384), BF),
            pltpu.VMEM((2, 16, 16, 384), BF),
            pltpu.VMEM((OWNERS, 16, 256), BF),
            pltpu.VMEM((16, 16, 256), BF),
            pltpu.VMEM((16, 16, 256), BF),
            pltpu.VMEM((OWNERS, 16, 256), BF),
            pltpu.SemaphoreType.DMA((N_SEND,)),
            pltpu.SemaphoreType.DMA((N_RECV,)),
            pltpu.SemaphoreType.DMA((4,)),
        ],
        compiler_params=pltpu.CompilerParams(
            collective_id=0, has_side_effects=True, vmem_limit_bytes=58 * 2**20
        ),
        name="soft_moe_backward",
    )(patches, cotangent, other_logsum, slot_keys, jnp.swapaxes(w_in, 1, 2), w_out)
    patch_grad, key_grad, w_in_grad, w_out_grad = pl.pallas_call(
        write_out,
        out_shape=[jax.ShapeDtypeStruct(r.shape, r.dtype) for r in results],
        in_specs=[any_spec] * 4,
        out_specs=[any_spec] * 4,
        scratch_shapes=[pltpu.SemaphoreType.DMA((4,))],
        compiler_params=pltpu.CompilerParams(vmem_limit_bytes=8 * 2**20),
        name="write_out",
    )(*results)
    return (patch_grad, key_grad, jnp.swapaxes(w_in_grad, 1, 2), w_out_grad)


def solution(mesh):
    placed = (
        P(("dp", "expert"), None, None),
        P(("dp", "expert"), None, None),
        P(("dp", "expert"), None),
        P(),
        P("expert", None, "dp"),
        P("expert", "dp", None),
    )
    return jax.shard_map(
        on_device,
        mesh=mesh,
        in_specs=placed,
        out_specs=(
            P(("dp", "expert"), None, None),
            P(),
            P("expert", None, "dp"),
            P("expert", "dp", None),
        ),
        check_vma=False,
    )
```

```python
import functools

import jax
import jax.numpy as jnp
from jax import lax
from jax.experimental import pallas as pl
from jax.experimental.pallas import tpu as pltpu
from jax.sharding import PartitionSpec as P

MESH = pl.DeviceIdType.MESH
BF = jnp.bfloat16
F32 = jnp.float32

D = 1280
FB = 320
SPLIT = 1024
COLS = {"A": (0, SPLIT), "B": (SPLIT, D - SPLIT)}
N_RECV = 80
N_SEND = 12
WINDOWS = (0, 384, 768, 896)
OWNERS = 10
GELU_C = 0.7978845608028654
GELU_A = 0.044715

ORDER = (
    ("a_got", 0), ("ag2", "A", 0, 0), ("ag1", "A", 0), ("a_got", 1), ("ag2", "A", 1, 0), ("ag1", "A", 1),
    ("ag1", "B", 1), ("ag1", "B", 0), ("ag2_relay", "A", 0, 0), ("ag2_relay", "A", 1, 0), ("ag1_relay", "B", 1),
    ("ag1_relay", "A", 0), ("ag1_relay", "B", 0), ("ag2", "A", 0, 1), ("ag2", "A", 0, 3), ("ag2", "B", 0, 3),
    ("ag1_relay", "A", 1), ("ag2", "A", 1, 1), ("ag2", "A", 0, 2), ("ag2", "B", 1, 3), ("ag2", "B", 0, 2),
    ("ag2", "B", 0, 1), ("ag2_relay", "A", 0, 1), ("ag2", "B", 1, 1), ("ag2", "B", 0, 0), ("ag2", "A", 1, 3),
    ("ag2_relay", "B", 1, 3), ("ag2", "A", 1, 2), ("ag2_relay", "B", 0, 1), ("ag2_relay", "B", 0, 3),
    ("ag2_relay", "A", 1, 1), ("ag2_relay", "A", 0, 3), ("ag2", "B", 1, 0), ("ag2_relay", "A", 0, 2),
    ("ag2", "B", 1, 2), ("ag2_relay", "B", 0, 0), ("ag2_relay", "B", 0, 2), ("ag2_relay", "B", 1, 1),
    ("expert", 0, 3), ("ag2_relay", "A", 1, 3), ("expert", 0, 1), ("ag2_relay", "B", 1, 0), ("rs1_u", "A", 0, 3),
    ("ag2_relay", "A", 1, 2), ("rs1_u", "A", 0, 2), ("ag2_relay", "B", 1, 2), ("expert", 0, 0), ("expert", 0, 2),
    ("rs1_t", "B", 0), ("rs1_t", "A", 0, 1), ("rs1_u", "B", 0), ("expert", 1, 1), ("rs1_t", "A", 0, 3),
    ("expert", 1, 0), ("rs1_t", "A", 0, 2), ("expert", 1, 2), ("expert", 1, 3), ("rs1_t", "A", 1, 2),
    ("rs1_t", "B", 1), ("rs1_t", "A", 1, 1), ("rs1_m", "B", 0), ("weight_grads", 0), ("rs1_u", "A", 0, 1),
    ("rs1_u", "A", 1, 2), ("rs1_m", "A", 0, 2), ("rs1_u", "B", 1), ("rs1_t", "A", 1, 3), ("rs1_m", "B", 1),
    ("rs1_m", "A", 1, 2), ("rs1_m", "A", 0, 1), ("rs1_m", "A", 0, 3), ("rs1_m", "A", 1, 1), ("rs1_f", "B", 0),
    ("rs1_u", "A", 1, 1), ("rs1_f", "A", 0, 2), ("rs2_t", "A", 0), ("rs1_f", "A", 1, 2), ("rs2_t", "A", 1),
    ("rs2_t", "B", 0), ("rs1_m", "A", 1, 3), ("rs1_f", "A", 0, 3), ("rs1_f", "B", 1), ("rs1_f", "A", 0, 1),
    ("rs2_u", "A", 0), ("rs1_u", "A", 1, 3), ("rs2_u", "B", 0), ("rs1_t", "A", 0, 0), ("rs1_t", "A", 1, 0),
    ("rs1_u", "A", 0, 0), ("rs2_m", "A", 0), ("rs2_t", "B", 1), ("rs1_f", "A", 1, 1), ("rs1_f", "A", 1, 3),
    ("rs2_u", "A", 1), ("rs2_m", "B", 0), ("rs1_m", "A", 0, 0), ("rs2_m", "A", 1), ("rs1_m", "A", 1, 0),
    ("rs1_u", "A", 1, 0), ("rs2_m", "B", 1), ("rs2_u", "B", 1), ("rs2_f", "B", 0), ("rs1_f", "A", 0, 0),
    ("rs2_f", "A", 0), ("b_send", 0), ("rs1_f", "A", 1, 0), ("rs2_f", "A", 1), ("rs2_f", "B", 1), ("b_send", 1),
    ("weight_grads", 1),
)


def dot(a, b):
    return lax.dot_general(a, b, (((1,), (0,)), ((), ())), preferred_element_type=F32)


def dot_nt(a, b):
    return lax.dot_general(a, b, (((1,), (1,)), ((), ())), preferred_element_type=F32)


def dot_tn(a, b):
    return lax.dot_general(a, b, (((0,), (0,)), ((), ())), preferred_element_type=F32)


def iota(shape, dim):
    return lax.broadcasted_iota(jnp.int32, shape, dim)


def piece_parts(r):
    return r >> 4, (r >> 2) & 3, (r >> 1) & 1, r & 1


def one_hot(index_of, window, others, pieces_first):
    shape = (256, others) if pieces_first else (others, 256)
    piece = iota(shape, 0 if pieces_first else 1)
    other = iota(shape, 1 if pieces_first else 0)
    hit = (index_of(piece) == other) & (piece_parts(piece)[1] == window)
    return jnp.where(hit, 1.0, 0.0).astype(BF)


def kernel(
    patches_hbm, cot_hbm, ols_ref, keys_ref, win_hbm, wout_hbm,
    pg, kg_ref, wig, wog,
    patches, cot, win, wout,
    disp_s, comb_s, g, pt, act_s, pre_s, r1, r2,
    a2s, a2r, b2s, b2r, ks, k1, k2, k3,
    hot_out, hot_in, hot_ret, hot_back,
    send_sem, recv_sem, in_sem,
):
    dp = lax.axis_index("dp")
    me = lax.axis_index("expert")
    zh, y = dp // 4, dp % 4

    def expert_peer(off):
        return (dp, lax.rem(me + off, 16))

    def dp_peer(off):
        return (lax.rem(dp + off, 16), me)

    def ring_peer(axis, step):
        if axis == "y":
            return (zh * 4 + lax.rem(y + step + 4, 4), me)
        return (lax.rem(zh + step + 4, 4) * 4 + y, me)

    barrier = pltpu.get_barrier_semaphore()
    for off in range(1, 16):
        pl.semaphore_signal(barrier, inc=1, device_id=expert_peer(off), device_id_type=MESH)
        pl.semaphore_signal(barrier, inc=1, device_id=dp_peer(off), device_id_type=MESH)

    loads = {}
    for n, (name, src, dst) in enumerate((
        ("x0", patches_hbm.at[0], patches.at[0]), ("x1", patches_hbm.at[1], patches.at[1]),
        ("c0", cot_hbm.at[0], cot.at[0]), ("c1", cot_hbm.at[1], cot.at[1]),
        ("wi", win_hbm, win), ("wo", wout_hbm, wout),
    )):
        loads[name] = pltpu.make_async_copy(src, dst, in_sem.at[n])
        if n < 4:
            loads[name].start()

    recv_of, send_of, waited = {}, {}, set()

    def send(group, out, src, dst, device):
        n = recv_of.setdefault(group, len(recv_of))
        m = send_of.setdefault(out, len(send_of))
        assert n < N_RECV and m < N_SEND
        pltpu.make_async_remote_copy(
            src_ref=src, dst_ref=dst, send_sem=send_sem.at[m], recv_sem=recv_sem.at[n],
            device_id=device, device_id_type=MESH,
        ).start()

    def total_of(ref, n, m):
        return pltpu.make_async_remote_copy(
            src_ref=ref, dst_ref=ref, send_sem=send_sem.at[m], recv_sem=recv_sem.at[n],
            device_id=expert_peer(1), device_id_type=MESH,
        )

    def got(group, ref):
        if group not in waited:
            waited.add(group)
            total_of(ref, recv_of[group], 0).wait_recv()

    def sent(out, ref):
        total_of(ref, 0, send_of.pop(out)).wait_send()

    def spread(k):
        def index(r):
            off, _, t, i = piece_parts(r)
            return (t * 2 + i) * 32 + 2 * ((me + off) & 15) + k

        return index

    def in_block(r):
        off, _, t, i = piece_parts(r)
        return t * 32 + off * 2 + i

    def spread_hots(k):
        for w in range(4):
            hot_out[4 * k + w] = one_hot(spread(k), w, 128, True)

    spread_hots(0)
    keys = keys_ref[...]
    rows_in, rows_grad, combines = [], [], []
    for i in range(2):
        loads["x%d" % i].wait()
        exponent = jnp.exp(dot_nt(keys, patches[i]))
        dispatch = exponent / jnp.sum(exponent, axis=1, keepdims=True)
        combine = exponent / (jnp.sum(exponent, axis=0, keepdims=True) + jnp.exp(ols_ref[i : i + 1, :]))
        disp_s[i] = dispatch
        comb_s[i] = combine
        rows_in.append(dot(dispatch.astype(BF), patches[i]).astype(BF))
        combines.append(combine.astype(BF))
    for i in range(2):
        loads["c%d" % i].wait()
        rows_grad.append(dot(combines[i], cot[i]).astype(BF))
    loads["wi"].start()
    loads["wo"].start()
    rows = jnp.concatenate(rows_in + rows_grad, axis=0)

    def to_pieces(rows, hots, dst):
        total = jnp.zeros((256, 384), F32)
        for w, c0 in enumerate(WINDOWS):
            total = total + dot(hots[w], rows[:, c0 : c0 + 384])
        dst[...] = total.astype(BF).reshape(16, 16, 384)

    pl.semaphore_wait(barrier, 30)
    for k in range(2):
        if k == 1:
            spread_hots(1)
        to_pieces(rows, hot_out.at[pl.ds(4 * k, 4)], a2s.at[k])
        a2r[k, 0] = a2s[k, 0]
        for off in range(1, 16):
            send(("a", k), ("a", k), a2s.at[k, off], a2r.at[k, off], expert_peer(off))
    for w in range(4):
        hot_in[w] = one_hot(in_block, w, 64, False)
        hot_ret[w] = one_hot(in_block, w, 64, True)
        for k in range(2):
            hot_back[4 * k + w] = one_hot(spread(k), w, 128, False)

    def a_got(k):
        got(("a", k), a2r.at[k, pl.ds(1, 15)])
        for w, c0 in enumerate(WINDOWS):
            block = dot(hot_in[w], a2r[k].reshape(256, 384)).astype(BF)
            if w == 3:
                block, c0 = block[:, 256:], c0 + 256
            g[2 * k : 2 * k + 2, 0, 0, :, c0 : c0 + block.shape[1]] = block.reshape(2, 32, block.shape[1])

    def b_send(k):
        to_pieces(pt[2 * k : 2 * k + 2, 0, 0].reshape(64, D), hot_ret, b2s.at[k])
        b2r[k, 0] = b2s[k, 0]
        for off in range(1, 16):
            send(("b", k), ("b", k), b2s.at[k, off], b2r.at[k, off], expert_peer(16 - off))

    AXES = {"A": ("z", "y"), "B": ("y", "z")}

    def cols_of(part):
        return pl.ds(*COLS[part])

    def at(ref, part, k, a1, a2, r0=0, nr=32):
        dy, dz = (a2, a1) if part == "A" else (a1, a2)
        return ref.at[pl.ds(2 * k, 2), dy, dz, pl.ds(r0, nr), cols_of(part)]

    def two(part, k):
        return g.at[pl.ds(2 * k, 2), 0, pl.ds(0, 2), :, cols_of(part)]

    def ag1(part, k):
        for step, a in ((1, 3), (-1, 1)):
            send(("p1", part, k), "ag1", at(g, part, k, 0, 0), at(g, part, k, a, 0), ring_peer(AXES[part][0], step))

    def ag1_relay(part, k):
        got(("p1", part, k), two(part, k))
        for step, a, r in ((1, 3, 0), (-1, 1, 16)):
            send(("r1", part, k), "ag1", at(g, part, k, a, 0, r, 16), at(g, part, k, 2, 0, r, 16), ring_peer(AXES[part][0], step))

    def first_in(part, k, a1):
        if a1 in (1, 3):
            got(("p1", part, k), two(part, k))
        if a1 == 2:
            got(("r1", part, k), at(g, part, k, 2, 0))

    def ag2(part, k, a1):
        first_in(part, k, a1)
        for step, a in ((1, 3), (-1, 1)):
            send(("p2", part, k, a1), "ag2", at(g, part, k, a1, 0), at(g, part, k, a1, a), ring_peer(AXES[part][1], step))

    def ag2_relay(part, k, a1):
        got(("p2", part, k, a1), two(part, k))
        for step, a, r in ((1, 3, 0), (-1, 1, 16)):
            send(("r2", part, k, a1), "ag2", at(g, part, k, a1, a, r, 16), at(g, part, k, a1, 2, r, 16), ring_peer(AXES[part][1], step))

    def slot_in(part, k, a1, a2):
        if a2 == 0:
            first_in(part, k, a1)
        elif a2 == 2:
            got(("r2", part, k, a1), at(g, part, k, a1, 2))
        else:
            got(("p2", part, k, a1), two(part, k))

    def expert(k, dy):
        for n in range(4):
            slot_in("A", k, n, dy)
            slot_in("B", k, dy, n)
        if "w" not in waited:
            waited.add("w")
            loads["wi"].wait()
            loads["wo"].wait()
        x0 = g[2 * k, dy].reshape(128, D)
        x1 = g[2 * k + 1, dy].reshape(128, D)
        hidden = dot_nt(x0, win[k])
        upstream = dot_nt(x1, wout[k])
        square = hidden * hidden
        tanh = jnp.tanh(GELU_C * (hidden + GELU_A * square * hidden))
        act = (0.5 * hidden * (1.0 + tanh)).astype(BF)
        slope = 0.5 * (1.0 + tanh) + (0.5 * hidden) * (1.0 - tanh * tanh) * (
            GELU_C + (3.0 * GELU_C * GELU_A) * square
        )
        pre = (slope * upstream).astype(BF)
        act_s[k, dy * 128 : dy * 128 + 128, :] = act
        pre_s[k, dy * 128 : dy * 128 + 128, :] = pre
        pt[2 * k, dy] = dot(act, wout[k]).astype(BF).reshape(4, 32, D)
        pt[2 * k + 1, dy] = dot(pre, win[k]).astype(BF).reshape(4, 32, D)

    def weight_grads(k):
        wog[k] = dot_tn(act_s[k], g[2 * k + 1].reshape(512, D)).astype(BF)
        wig[k] = dot_tn(pre_s[k], g[2 * k].reshape(512, D)).astype(BF)

    TP, TM, UP, MP, UM, MM = range(6)

    def part_of(ph, part, k, a1, a2, r0):
        if ph == 1 and part == "B":
            return pt.at[pl.ds(2 * k, 2), :, a2, pl.ds(r0, 16), cols_of(part)]
        if ph == 1:
            return at(pt, part, k, a1, a2, r0, 16)
        return at(pt, part, k, a2, 0, r0, 16)

    def land(ph, part, k, a1, m):
        if ph == 1:
            return r1.at[k, m, :, slice(None) if part == "B" else a1, :, cols_of(part)]
        return r2.at[k, m, :, :, cols_of(part)]

    def rs_send(ph, part, k, a1, m, a2, r0):
        step = 1 if m in (TP, UP, MP) else -1
        kind = "t" if m < 2 else "u"
        send((kind, ph, part, k, a1), ("rs", ph), part_of(ph, part, k, a1, a2, r0), land(ph, part, k, a1, m), ring_peer(AXES[part][2 - ph], step))

    def rs_got(ph, part, k, a1, kind):
        m = pl.ds(0, 2) if kind == "t" else pl.ds(2, 4)
        got((kind, ph, part, k, a1), land(ph, part, k, a1, m))

    def rs_t(ph, part, k, a1=None):
        rs_send(ph, part, k, a1, TP, 2, 16)
        rs_send(ph, part, k, a1, TM, 2, 0)

    def rs_u(ph, part, k, a1=None):
        rs_send(ph, part, k, a1, UP, 1, 0)
        rs_send(ph, part, k, a1, UM, 3, 16)

    def add_into(dst, *srcs):
        total = dst[...].astype(F32)
        for src in srcs:
            total = total + src[...].astype(F32)
        dst[...] = total.astype(BF)

    def rs_m(ph, part, k, a1=None):
        rs_got(ph, part, k, a1, "t")
        for t, m, a2, r0 in ((TP, MP, 1, 16), (TM, MM, 3, 0)):
            add_into(part_of(ph, part, k, a1, a2, r0), land(ph, part, k, a1, t))
            rs_send(ph, part, k, a1, m, a2, r0)

    def rs_f(ph, part, k, a1=None):
        rs_got(ph, part, k, a1, "u")
        for u, m, r0 in ((UP, MM, 0), (UM, MP, 16)):
            add_into(part_of(ph, part, k, a1, 0, r0), land(ph, part, k, a1, u), land(ph, part, k, a1, m))

    steps = {"ag1": ag1, "ag1_relay": ag1_relay, "ag2": ag2, "ag2_relay": ag2_relay, "expert": expert, "weight_grads": weight_grads, "a_got": a_got, "b_send": b_send}
    for ph in (1, 2):
        for name, step in (("t", rs_t), ("u", rs_u), ("m", rs_m), ("f", rs_f)):
            steps["rs%d_%s" % (ph, name)] = functools.partial(step, ph)
    for name, *where in ORDER:
        steps[name](*where)

    back = [jnp.zeros((128, 384), F32)] * 4
    for k in range(2):
        got(("b", k), b2r.at[k, pl.ds(1, 15)])
        pieces = b2r[k].reshape(256, 384)
        back = [back[w] + dot(hot_back[4 * k + w], pieces) for w in range(4)]
    back[3] = back[3][:, 256:]
    back = jnp.concatenate([b.astype(BF) for b in back], axis=1)

    halves = []
    key_part = jnp.zeros((32, D), F32)
    for i in range(2):
        slot_out = back[i * 32 : i * 32 + 32]
        slot_in_grad = back[64 + i * 32 : 96 + i * 32]
        comb_grad = dot_nt(slot_out, cot[i])
        disp_grad = dot_nt(slot_in_grad, patches[i])
        dispatch = disp_s[i]
        combine = comb_s[i]
        logit_grad = combine * (comb_grad - jnp.sum(combine * comb_grad, axis=0, keepdims=True))
        logit_grad = logit_grad + dispatch * (
            disp_grad - jnp.sum(dispatch * disp_grad, axis=1, keepdims=True)
        )
        logit_half = logit_grad.astype(BF)
        key_part = key_part + dot(logit_half, patches[i])
        halves.append((dispatch.astype(BF), logit_half, slot_in_grad))

    def piece(o):
        return slice(o // 5 * 16, o // 5 * 16 + 16), slice(o % 5 * 256, o % 5 * 256 + 256)

    owner = me < OWNERS
    for o in range(OWNERS):
        ks[o] = key_part[piece(o)].astype(BF)

        @pl.when(me != o)
        def _():
            send("k1", "k1", ks.at[o], k1.at[me], (dp, o))

    def image_out(i):
        dispatch_half, logit_half, slot_in_grad = halves[i]
        lhs = jnp.concatenate([dispatch_half, logit_half], axis=0)
        rhs = jnp.concatenate([slot_in_grad, keys], axis=0)
        pg[i] = dot_tn(lhs, rhs).astype(BF)

    image_out(0)

    @pl.when(owner)
    def _():
        k1[me] = ks[me]
        got("k1", k1.at[pl.ds(1, 15)])
        total = k1[0].astype(F32)
        for n in range(1, 16):
            total = total + k1[n].astype(F32)
        k2[dp] = total.astype(BF)
        for off in range(1, 16):
            send("k2", "k2", k2.at[dp], k2.at[dp], dp_peer(off))

    image_out(1)

    @pl.when(owner)
    def _():
        got("k2", k2.at[pl.ds(1, 15)])
        total = k2[0].astype(F32)
        for n in range(1, 16):
            total = total + k2[n].astype(F32)
        k3[me] = total.astype(BF)
        for off in range(1, 16):
            send("k3", "k3", k3.at[me], k3.at[me], expert_peer(off))

    n_k1, n_k3 = send_of["k1"], recv_of["k3"]
    waited.add("k3")

    @pl.when(owner)
    def _():
        total_of(k3.at[pl.ds(0, OWNERS - 1)], n_k3, 0).wait_recv()

    @pl.when(jnp.logical_not(owner))
    def _():
        total_of(k3, n_k3, 0).wait_recv()

    for o in range(OWNERS):
        kg_ref[piece(o)] = k3[o].astype(F32)

    @pl.when(owner)
    def _():
        total_of(ks.at[pl.ds(0, OWNERS - 1)], 0, n_k1).wait_send()
        sent("k2", k2.at[pl.ds(1, 15)])
        sent("k3", k1.at[pl.ds(1, 15)])

    @pl.when(jnp.logical_not(owner))
    def _():
        total_of(ks, 0, send_of.pop("k1")).wait_send()

    for k in range(2):
        sent(("a", k), a2s.at[k, pl.ds(1, 15)])
        sent(("b", k), b2s.at[k, pl.ds(1, 15)])
    sent("ag1", g.at[:, 0, pl.ds(1, 3)])
    sent("ag2", g.at[:, pl.ds(1, 3)])
    sent(("rs", 1), r1)
    sent(("rs", 2), r2)
    assert not send_of and len(waited) == len(recv_of) + 1


def write_out(*refs):
    copies = [pltpu.make_async_copy(refs[n], refs[n + 4], refs[8].at[n]) for n in range(4)]
    for copy in copies:
        copy.start()
    for copy in copies:
        copy.wait()


def on_device(patches, cotangent, other_logsum, slot_keys, w_in, w_out):
    any_spec = pl.BlockSpec(memory_space=pl.ANY)
    vmem = pl.BlockSpec(memory_space=pltpu.VMEM)
    results = pl.pallas_call(
        kernel,
        out_shape=(
            pltpu.VMEM((2, 256, D), BF),
            pltpu.VMEM((32, D), F32),
            pltpu.VMEM((2, FB, D), BF),
            pltpu.VMEM((2, FB, D), BF),
        ),
        in_specs=[any_spec, any_spec, vmem, vmem, any_spec, any_spec],
        out_specs=(vmem, vmem, vmem, vmem),
        scratch_shapes=[
            pltpu.VMEM((2, 256, D), BF),
            pltpu.VMEM((2, 256, D), BF),
            pltpu.VMEM((2, FB, D), BF),
            pltpu.VMEM((2, FB, D), BF),
            pltpu.VMEM((2, 32, 256), F32),
            pltpu.VMEM((2, 32, 256), F32),
            pltpu.VMEM((4, 4, 4, 32, D), BF),
            pltpu.VMEM((4, 4, 4, 32, D), BF),
            pltpu.VMEM((2, 512, FB), BF),
            pltpu.VMEM((2, 512, FB), BF),
            pltpu.VMEM((2, 6, 2, 4, 16, D), BF),
            pltpu.VMEM((2, 6, 2, 16, D), BF),
            pltpu.VMEM((2, 16, 16, 384), BF),
            pltpu.VMEM((2, 16, 16, 384), BF),
            pltpu.VMEM((2, 16, 16, 384), BF),
            pltpu.VMEM((2, 16, 16, 384), BF),
            pltpu.VMEM((OWNERS, 16, 256), BF),
            pltpu.VMEM((16, 16, 256), BF),
            pltpu.VMEM((16, 16, 256), BF),
            pltpu.VMEM((OWNERS, 16, 256), BF),
            pltpu.VMEM((8, 256, 128), BF),
            pltpu.VMEM((4, 64, 256), BF),
            pltpu.VMEM((4, 256, 64), BF),
            pltpu.VMEM((8, 128, 256), BF),
            pltpu.SemaphoreType.DMA((N_SEND,)),
            pltpu.SemaphoreType.DMA((N_RECV,)),
            pltpu.SemaphoreType.DMA((6,)),
        ],
        compiler_params=pltpu.CompilerParams(
            collective_id=0, has_side_effects=True, vmem_limit_bytes=58 * 2**20
        ),
        name="soft_moe_backward",
    )(patches, cotangent, other_logsum, slot_keys, jnp.swapaxes(w_in, 1, 2), w_out)
    patch_grad, key_grad, w_in_grad, w_out_grad = pl.pallas_call(
        write_out,
        out_shape=[jax.ShapeDtypeStruct(r.shape, r.dtype) for r in results],
        in_specs=[any_spec] * 4,
        out_specs=[any_spec] * 4,
        scratch_shapes=[pltpu.SemaphoreType.DMA((4,))],
        compiler_params=pltpu.CompilerParams(vmem_limit_bytes=8 * 2**20),
        name="write_out",
    )(*results)
    return (patch_grad, key_grad, jnp.swapaxes(w_in_grad, 1, 2), w_out_grad)


def solution(mesh):
    placed = (
        P(("dp", "expert"), None, None),
        P(("dp", "expert"), None, None),
        P(("dp", "expert"), None),
        P(),
        P("expert", None, "dp"),
        P("expert", "dp", None),
    )
    return jax.shard_map(
        on_device,
        mesh=mesh,
        in_specs=placed,
        out_specs=(
            P(("dp", "expert"), None, None),
            P(),
            P("expert", None, "dp"),
            P("expert", "dp", None),
        ),
        check_vma=False,
    )
```
